512 devices in a mesh: patch: 64 (over z, y_hi, core), head: 8 (over y_lo, x).
Axes of the slice: x: 4, y: 8 (y_hi: 4, y_lo: 2; y = y_hi * 2 + y_lo), z: 8, core: 2. Of those that a mesh axis runs over, the one named last changes fastest.
Arguments:
- fresh_query: bfloat16 [6144, 4096], P(('patch', 'head')), may hold values from -128 to 128
- fresh_key: bfloat16 [6144, 4096], P(('patch', 'head')), may hold values from -6 to 6
- fresh_value: bfloat16 [6144, 4096], P(('patch', 'head')), may hold values from -6 to 6
- stale_key: bfloat16 [6144, 4096], P('patch', 'head'), may hold values from -4 to 4
- stale_value: bfloat16 [6144, 4096], P('patch', 'head'), may hold values from -6 to 6
- lengths: int32 [64], replicated, may hold values from 1 to 96, 4608 in all
- hidden: bfloat16 [6144, 3072], P(('patch', 'head')), may hold values from -4 to 4
- gate_scale: float32 [3072], replicated, may hold values from 0.1 to 1.9
- out_weight: bfloat16 [4096, 3072], P('head'), may hold values from -0.09375 to 0.09375
Outputs:
- mixed: bfloat16 [6144, 3072], P(('patch', 'head'))
The draws below stay inside these ranges and needn't reach their ends.
Inputs may be any that keep to these rules, and one draw needn't show every extreme that they name: Slot j of patch p is live when j < lengths[p]; some patch is full in every draw; the lengths sum to 4608.
All inputs are finite; a program needn't handle non-finite values.
Results may differ from the reference program's by a relative error of at most 0.013.
Values may be sent and summed in bfloat16 or wider, within the bound.
No kernel may reach another device: no remote copies, remote signals or barrier semaphores. Data moves between devices by JAX's collectives and lax.ppermute only.
A program may use at most 64 MiB of HBM per device.

```python
import math
import jax
import jax.numpy as jnp
import numpy as np
from jax import lax

D = 3072
HD = 128
HEADS = 32
CAP = 96
TOKENS = 6144
N_PATCH = 64
N_HEAD = 8


def shared_base(key):
    return jnp.clip(jax.random.normal(key, (TOKENS, HEADS * HD), jnp.float32), -4.0, 4.0)


def draw_fresh_query(key, part):
    key = jax.random.fold_in(key, 11)
    values = jnp.clip(2.0 * jax.random.normal(key, (TOKENS, HEADS * HD), jnp.float32), -8.0, 8.0)
    return values.astype(jnp.bfloat16)


def draw_stale_key(key, part):
    base = shared_base(key)
    values = base
    return values.astype(jnp.bfloat16)


def levels(rng, shape, pieces, least, largest):
    loudness = 1.0
    for position, blocks in pieces:
        heights = jax.random.uniform(jax.random.fold_in(jax.random.fold_in(rng, 6), position), (blocks,), jnp.float32, least / len(pieces), largest / len(pieces))
        loudness = loudness * jnp.repeat(jnp.exp(heights), shape[position] // blocks).reshape((-1,) + (1,) * (len(shape) - 1 - position))
    return loudness


def profile(amount, total, most, lean):
    portions = [(1 << 20) // math.isqrt(rank ** lean) + 1 for rank in range(2, amount + 1)]
    spare, holding = total - most - (amount - 1), [1] * (amount - 1)
    while spare > 0:
        movable = [i for i in range(amount - 1) if holding[i] < most]
        mass, left = sum([portions[i] for i in movable]), spare
        for i in movable:
            more = min(most - holding[i], max(1, left * portions[i] // mass), spare)
            holding[i] = holding[i] + more
            spare = spare - more
    return np.array([most] + holding)


def ragged_sizes(rng, number_of, total, most, slope):
    if number_of == 2:
        one = jax.random.randint(rng, (), max(1, total - most), min(most, total - 1) + 1)
        return jnp.stack([one, total - one])
    sizes = jnp.asarray(profile(number_of, total, most, slope), jnp.int32)
    twos = (number_of - 1) // 2
    giver, receiver = sizes[1:1 + 2 * twos:2], sizes[2:2 + 2 * twos:2]
    margin = jnp.minimum(giver - 1, most - receiver)
    moved = jax.random.randint(jax.random.fold_in(rng, 1), (twos,), 0, 1 << 20) % (margin + 1)
    sizes = sizes.at[1:1 + 2 * twos:2].set(giver - moved).at[2:2 + 2 * twos:2].set(receiver + moved)
    return sizes[jax.random.permutation(jax.random.fold_in(rng, 2), number_of)]


def centred(rng, dims, deviation, reach, pieces=(), held_as=jnp.bfloat16):
    level = levels(rng, dims, pieces, -0.22, 0.18) if pieces else 1.0
    drawn = jax.random.normal(rng, dims, jnp.float32) * deviation * level
    return jnp.minimum(jnp.maximum(drawn, -reach), reach).astype(held_as)


def setup_inputs(seed: int = 0) -> dict:
    key_of = jax.random.split(jax.random.key(seed), 10)
    return {
        "fresh_query": draw_fresh_query(jax.random.fold_in(key_of[9], 71), 0),
        "fresh_key": centred(key_of[1], (TOKENS, HEADS * HD), 1.0, 6.0, ((0, 512),)),
        "fresh_value": centred(key_of[2], (TOKENS, HEADS * HD), 1.0, 6.0, ((0, 512),)),
        "stale_key": draw_stale_key(jax.random.fold_in(key_of[9], 71), 0),
        "stale_value": centred(key_of[4], (TOKENS, HEADS * HD), 1.0, 6.0, ((0, 64), (1, 8))),
        "lengths": ragged_sizes(key_of[5], N_PATCH, 3 * TOKENS // 4, CAP, 1).astype(jnp.int32),
        "hidden": centred(key_of[6], (TOKENS, D), 0.25, 4.0, ((0, 512),)),
        "gate_scale": jnp.clip(1.0 + 0.18 * jax.random.normal(key_of[7], (D,), jnp.float32), 0.1, 1.9),
        "out_weight": centred(key_of[8], (HEADS * HD, D), (HEADS * HD) ** -0.5, 0.09375, ((0, 8),)),
    }


negative_big = -1.0e30


def reference(fresh_query, fresh_key, fresh_value, stale_key, stale_value, lengths, hidden, gate_scale, out_weight):
    slot_ids = jnp.arange(CAP, dtype=jnp.int32)
    key_live = slot_ids[None, :] < lengths[:, None]
    same_patch = jnp.eye(N_PATCH, dtype=bool)[:, None, :, None]
    live_four = key_live[None, None, :, :]
    score_scale = HD ** -0.5

    def per_head(head_index):
        def columns(array):
            return lax.dynamic_slice_in_dim(array, head_index * HD, HD, 1)

        queries = columns(fresh_query)
        far_scores = jnp.dot(queries, columns(stale_key).T, preferred_element_type=jnp.float32)
        far_scores = far_scores.reshape(N_PATCH, CAP, N_PATCH, CAP) * score_scale
        query_three = queries.reshape(N_PATCH, CAP, HD).astype(jnp.float32)
        key_three = columns(fresh_key).reshape(N_PATCH, CAP, HD).astype(jnp.float32)
        near_scores = jnp.einsum("pid,pjd->pij", query_three, key_three) * score_scale
        scores = jnp.where(same_patch, near_scores[:, :, None, :], far_scores)
        row_top = jnp.max(jnp.where(live_four, scores, negative_big), axis=(2, 3), keepdims=True)
        weights = jnp.where(live_four, jnp.exp(scores - row_top), 0.0)
        denominator = jnp.sum(weights, axis=(2, 3))
        rounded = weights.astype(jnp.bfloat16)
        far_weights = jnp.where(same_patch, jnp.zeros((), jnp.bfloat16), rounded).reshape(TOKENS, TOKENS)
        far_part = jnp.dot(far_weights, columns(stale_value), preferred_element_type=jnp.float32)
        far_part = far_part.reshape(N_PATCH, CAP, HD)
        diagonal_blocks = jnp.transpose(jnp.diagonal(rounded, axis1=0, axis2=2), (2, 0, 1)).astype(jnp.float32)
        value_three = columns(fresh_value).reshape(N_PATCH, CAP, HD).astype(jnp.float32)
        near_part = jnp.einsum("pij,pjd->pid", diagonal_blocks, value_three)
        return ((far_part + near_part) / denominator[:, :, None]).reshape(TOKENS, HD)

    per_heads = lax.map(per_head, jnp.arange(HEADS, dtype=jnp.int32))
    attended = jnp.transpose(per_heads, (1, 0, 2)).reshape(TOKENS, HEADS * HD).astype(jnp.bfloat16)
    group_width = HEADS * HD // N_HEAD

    def add_group(total, group_index):
        cols = lax.dynamic_slice_in_dim(attended, group_index * group_width, group_width, 1)
        rows = lax.dynamic_slice_in_dim(out_weight, group_index * group_width, group_width, 0)
        partial_sum = jnp.dot(cols, rows, preferred_element_type=jnp.float32).astype(jnp.bfloat16)
        return total + partial_sum.astype(jnp.float32), None

    projected, _ = lax.scan(add_group, jnp.zeros((TOKENS, D), jnp.float32), jnp.arange(N_HEAD, dtype=jnp.int32))
    query_live = key_live.reshape(TOKENS)
    residual = hidden.astype(jnp.float32)
    mixed = jnp.where(query_live[:, None], residual + gate_scale[None, :] * projected, residual)
    return mixed.astype(jnp.bfloat16)
```

```python
import jax
import jax.numpy as jnp
import numpy as np
from jax import lax
from jax.experimental import pallas as pl
from jax.experimental.pallas import tpu as pltpu
from jax.sharding import Mesh, PartitionSpec as P

HD = 128
CAP = 96
NZ, NY, NC, NYL, NX = 8, 4, 2, 2, 4
NHEAD = NYL * NX
GROUP = 512
HEADS_HERE = GROUP // HD
OWN = 12
D = 3072
FAR = NZ * CAP
BIG = -1e30
EXP2_SCALE = float(np.log2(np.e) * HD ** (-0.5))
HEAD = ("yl", "x")
ALL = ("z", "yh", "c", "yl", "x")
f32 = jnp.float32
bf16 = jnp.bfloat16
PACKED = 3 * 768 // 2
OUT_PACKED = (D + D // 2) // 2


def params(mb):
    return pltpu.CompilerParams(vmem_limit_bytes=mb * 2**20)


def lower_half(shape):
    return lax.broadcasted_iota(jnp.int32, shape, 0) < 4


def pack_kernel(q_ref, k_ref, v_ref, out_ref):
    mask = lower_half((8, GROUP // 2))
    for h in range(NHEAD):
        tops, rests = [], []
        for ref in (q_ref, k_ref, v_ref):
            rows = ref[:, h * GROUP:(h + 1) * GROUP].astype(f32)
            tops.append(rows[0:8])
            tail = rows[4:12]
            first = pltpu.roll(tail[:, : GROUP // 2], 4, 0)
            rests.append(jnp.where(mask, first, tail[:, GROUP // 2:]))
        flat = jnp.concatenate(tops + rests, axis=1)
        both = jnp.concatenate([flat[:, :PACKED], flat[:, PACKED:]], axis=0)
        out_ref[h] = both.astype(bf16)


def pack(fq, fk, fv):
    return pl.pallas_call(
        pack_kernel,
        out_shape=jax.ShapeDtypeStruct((NHEAD, 16, PACKED), bf16),
        compiler_params=params(16),
    )(fq, fk, fv)


def row_tokens():
    top = [12 * s + r for s in range(8) for r in range(8)]
    rest = [12 * s + r for s in range(8) for r in range(8, 12)]
    return np.array(top + rest, np.int32)


def unpack_kernel(in_ref, q_ref, k_ref, v_ref):
    mask = lower_half((8, GROUP // 2))
    tops = [[], [], []]
    rests = [[], [], []]
    for s in range(NHEAD):
        both = in_ref[s].astype(f32)
        flat = jnp.concatenate([both[0:8], both[8:16]], axis=1)
        for i in range(3):
            tops[i].append(flat[:, i * GROUP:(i + 1) * GROUP])
            base = 3 * GROUP + i * (GROUP // 2)
            rests[i].append(flat[:, base:base + GROUP // 2])
    for i, ref in enumerate((q_ref, k_ref, v_ref)):
        tiles = list(tops[i])
        for k in range(NHEAD // 2):
            a, b = rests[i][2 * k], rests[i][2 * k + 1]
            left = jnp.where(mask, a, pltpu.roll(b, 4, 0))
            right = jnp.where(mask, pltpu.roll(a, 4, 0), b)
            tiles.append(jnp.concatenate([left, right], axis=1))
        ref[...] = jnp.concatenate(tiles, axis=0).astype(bf16)


def unpack(received):
    one = jax.ShapeDtypeStruct((CAP, GROUP), bf16)
    return pl.pallas_call(
        unpack_kernel, out_shape=(one, one, one), compiler_params=params(16)
    )(received)


def attention_kernel(q_ref, ka_ref, kb_ref, kf_ref, va_ref, vb_ref, vf_ref, bias_ref, out_ref):
    h = pl.program_id(0)
    lane = lax.broadcasted_iota(jnp.int32, (CAP, HD), 1)
    keys = (ka_ref[...], kb_ref[...], kf_ref[...])
    values = (va_ref[...], vb_ref[...], vf_ref[...])
    starts = (0, FAR, 2 * FAR)
    sizes = (FAR, FAR, CAP)
    for b in range(NY):
        query = q_ref[b]
        scores = []
        for key, start, size in zip(keys, starts, sizes):
            dot = lax.dot_general(query, key, (((1,), (1,)), ((), ())), preferred_element_type=f32)
            scores.append(dot + bias_ref[b, :, start:start + size])
        top = scores[0].max(axis=1, keepdims=True)
        for s in scores[1:]:
            top = jnp.maximum(top, s.max(axis=1, keepdims=True))
        total = jnp.zeros((CAP, 1), f32)
        accum = jnp.zeros((CAP, HD), f32)
        for s, value in zip(scores, values):
            weights = jnp.exp2((s - top) * EXP2_SCALE)
            total = total + weights.sum(axis=1, keepdims=True)
            accum = accum + jnp.dot(weights.astype(bf16), value, preferred_element_type=f32)
        out_ref[b, :, pl.ds(pl.multiple_of(h * HD, HD), HD)] = (accum / total).astype(bf16)
        level = top * EXP2_SCALE + jnp.log2(total)
        hi = level.astype(bf16).astype(f32)
        mid = (level - hi).astype(bf16).astype(f32)
        low = level - hi - mid
        stat = jnp.where(lane == 3 * h, hi, 0.0)
        stat = jnp.where(lane == 3 * h + 1, mid, stat)
        stat = jnp.where(lane == 3 * h + 2, low, stat).astype(bf16)

        @pl.when(h == 0)
        def _():
            out_ref[b, :, GROUP:] = stat

        @pl.when(h != 0)
        def _():
            out_ref[b, :, GROUP:] = out_ref[b, :, GROUP:] + stat


def attention(q, ka, kb, kf, va, vb, vf, bias):
    def column(rows):
        return pl.BlockSpec((rows, HD), lambda h: (0, h))

    return pl.pallas_call(
        attention_kernel,
        grid=(HEADS_HERE,),
        in_specs=[
            pl.BlockSpec((NY, CAP, HD), lambda h: (0, 0, h)),
            column(FAR), column(FAR), column(CAP), column(FAR), column(FAR), column(CAP),
            pl.BlockSpec((NY, 1, 2 * FAR + HD), lambda h: (0, 0, 0)),
        ],
        out_specs=pl.BlockSpec((NY, CAP, GROUP + HD), lambda h: (0, 0, 0)),
        out_shape=jax.ShapeDtypeStruct((NY, CAP, GROUP + HD), bf16),
        compiler_params=params(32),
        cost_estimate=pl.CostEstimate(
            flops=4 * NY * CAP * (2 * FAR + CAP) * GROUP,
            bytes_accessed=4 * 2 * FAR * GROUP * 2,
            transcendentals=NY * CAP * (2 * FAR + CAP) * HEADS_HERE,
        ),
    )(q, ka, kb, kf, va, vb, vf, bias)


def project_kernel(part_ref, w_ref, out_ref, w_vmem, sem):
    copy = pltpu.make_async_copy(w_ref, w_vmem, sem)
    copy.start()
    stats = [part_ref[b, :, GROUP:].astype(f32) for b in range(NY)]
    heads = []
    for h in range(HEADS_HERE):
        levels = [s[:, 3 * h:3 * h + 1] + s[:, 3 * h + 1:3 * h + 2] + s[:, 3 * h + 2:3 * h + 3] for s in stats]
        top = levels[0]
        for level in levels[1:]:
            top = jnp.maximum(top, level)
        total = jnp.zeros((CAP, 1), f32)
        accum = jnp.zeros((CAP, HD), f32)
        for b in range(NY):
            weight = jnp.exp2(levels[b] - top)
            total = total + weight
            accum = accum + weight * part_ref[b, :, h * HD:(h + 1) * HD].astype(f32)
        heads.append((accum / total).astype(bf16))
    attended = jnp.concatenate(heads, axis=1)
    copy.wait()
    half = D // 2
    step = 384
    mask = lower_half((8, step))
    for j in range(half // step):
        left = jnp.dot(attended, w_vmem[:, j * step:(j + 1) * step], preferred_element_type=f32)
        right = jnp.dot(attended, w_vmem[:, half + j * step:half + (j + 1) * step], preferred_element_type=f32)
        for s in range(NHEAD):
            k = s // 2
            a = left[64 + 8 * k:72 + 8 * k]
            b = right[64 + 8 * k:72 + 8 * k]
            if s % 2 == 0:
                rest = jnp.where(mask, a, pltpu.roll(b, 4, 0))
            else:
                rest = jnp.where(mask, pltpu.roll(a, 4, 0), b)
            pieces = (
                (j * step, left[8 * s:8 * s + 8]),
                (half + j * step, right[8 * s:8 * s + 8]),
                (D + j * step, rest),
            )
            for col, tile in pieces:
                row = 8 * (col // OUT_PACKED)
                col = col % OUT_PACKED
                assert col + step <= OUT_PACKED
                out_ref[s, row:row + 8, col:col + step] = tile.astype(bf16)


def project(parts, w):
    return pl.pallas_call(
        project_kernel,
        in_specs=[pl.BlockSpec(memory_space=pltpu.VMEM), pl.BlockSpec(memory_space=pl.ANY)],
        out_specs=pl.BlockSpec(memory_space=pltpu.VMEM),
        out_shape=jax.ShapeDtypeStruct((NHEAD, 16, OUT_PACKED), bf16),
        scratch_shapes=[pltpu.VMEM((GROUP, D), bf16), pltpu.SemaphoreType.DMA],
        compiler_params=params(24),
    )(parts, w)


def mix_kernel(limit_ref, in_ref, hidden_ref, gate_ref, out_ref):
    total = in_ref[0].astype(f32)
    for s in range(1, NHEAD):
        total = total + in_ref[s].astype(f32)
    flat = jnp.concatenate([total[0:8], total[8:16]], axis=1)
    half = D // 2
    rest = flat[:, D:]
    tail = jnp.concatenate([rest[0:4], rest[4:8]], axis=1)
    projected = jnp.concatenate([flat[:, :D], tail], axis=0)
    residual = hidden_ref[...].astype(f32)
    live = lax.broadcasted_iota(jnp.int32, (OWN, D), 0) < limit_ref[0]
    mixed = jnp.where(live, residual + gate_ref[...] * projected, residual)
    out_ref[...] = mixed.astype(bf16)


def mix(limit, received, hidden, gate):
    vmem = pl.BlockSpec(memory_space=pltpu.VMEM)
    return pl.pallas_call(
        mix_kernel,
        in_specs=[pl.BlockSpec(memory_space=pltpu.SMEM), vmem, vmem, vmem],
        out_specs=vmem,
        out_shape=jax.ShapeDtypeStruct((OWN, D), bf16),
        compiler_params=params(16),
    )(limit, received, hidden, gate)


def swap(x, axis):
    return lax.all_to_all(x, axis, split_axis=0, concat_axis=0, tiled=True)


def local(fq, fk, fv, sk, sv, lengths, hidden, gate, w):
    z, yh, c = (lax.axis_index(a) for a in ("z", "yh", "c"))
    own_head = lax.axis_index("yl") * NX + lax.axis_index("x")

    def spread(x):
        return swap(jnp.broadcast_to(x[None], (NZ, CAP, GROUP)), "z").reshape(FAR, GROUP)

    def other_core(x):
        return lax.ppermute(x, "c", [(0, 1), (1, 0)])

    ka, va = spread(sk), spread(sv)
    kb, vb = other_core(ka), other_core(va)
    query, kf, vf = unpack(swap(pack(fq, fk, fv), HEAD))
    queries = lax.all_gather(query, "yh", axis=0)

    table = lengths.reshape(NZ, NY, NC)
    mine = lax.dynamic_slice_in_dim(table, yh, 1, 1)[:, 0, :]
    own_core = jnp.where(c == 0, mine[:, 0], mine[:, 1])
    far_core = jnp.where(c == 0, mine[:, 1], mine[:, 0])
    own_length = jnp.sum(jnp.where(jnp.arange(NZ) == z, own_core, 0))
    slots = jnp.arange(CAP, dtype=jnp.int32)
    is_mine = (jnp.arange(NY) == yh)[:, None, None]
    stale_here = (jnp.arange(NZ) == z)[None, :, None]
    live_a = (slots[None, None, :] < own_core[None, :, None]) & ~(is_mine & stale_here)
    live_b = jnp.broadcast_to(slots[None, None, :] < far_core[None, :, None], (NY, NZ, CAP))
    live_f = (jnp.asarray(row_tokens())[None, :] < own_length) & is_mine[:, :, 0]
    live = jnp.concatenate([live_a.reshape(NY, FAR), live_b.reshape(NY, FAR), live_f, jnp.zeros((NY, HD - CAP), bool)], axis=1)
    bias = jnp.where(live, 0.0, BIG).astype(f32)[:, None, :]

    parts = attention(queries, ka, kb, kf, va, vb, vf, bias)
    packed = project(swap(parts, "yh"), w)
    limit = jnp.clip(own_length - own_head * OWN, 0, OWN)[None]
    return mix(limit, swap(packed, HEAD), hidden, gate[None, :])


def solution(mesh):
    grid = Mesh(mesh.devices.reshape(NZ, NY, NC, NYL, NX), ALL)
    rows = P(ALL, None)
    stale = P(("z", "yh", "c"), HEAD)
    in_specs = (rows, rows, rows, stale, stale, P(), rows, P(), P(HEAD, None))
    return jax.shard_map(local, mesh=grid, in_specs=in_specs, out_specs=rows, check_vma=False)
```

```python
import jax
import jax.numpy as jnp
import numpy as np
from jax import lax
from jax.experimental import pallas as pl
from jax.experimental.pallas import tpu as pltpu
from jax.sharding import Mesh, PartitionSpec as P

HD = 128
CAP = 96
NZ, NY, NC, NYL, NX = 8, 4, 2, 2, 4
NHEAD = NYL * NX
GROUP = 512
HEADS_HERE = GROUP // HD
OWN = 12
D = 3072
KEYS = NZ * NC * CAP
QUERIES = NY * CAP
BIG = -1e30
EXP2_SCALE = float(np.log2(np.e) * HD ** (-0.5))
HEAD = ("yl", "x")
ALL = ("z", "yh", "c", "yl", "x")
f32 = jnp.float32
bf16 = jnp.bfloat16
PACKED = 3 * 768 // 2
OUT_PACKED = (D + D // 2) // 2


def params(mb):
    return pltpu.CompilerParams(vmem_limit_bytes=mb * 2**20)


def lower_half(shape):
    return lax.broadcasted_iota(jnp.int32, shape, 0) < 4


def pack_kernel(q_ref, k_ref, v_ref, out_ref):
    mask = lower_half((8, GROUP // 2))
    for h in range(NHEAD):
        tops, rests = [], []
        for ref in (q_ref, k_ref, v_ref):
            rows = ref[:, h * GROUP:(h + 1) * GROUP].astype(f32)
            tops.append(rows[0:8])
            tail = rows[4:12]
            first = pltpu.roll(tail[:, : GROUP // 2], 4, 0)
            rests.append(jnp.where(mask, first, tail[:, GROUP // 2:]))
        flat = jnp.concatenate(tops + rests, axis=1)
        both = jnp.concatenate([flat[:, :PACKED], flat[:, PACKED:]], axis=0)
        out_ref[h] = both.astype(bf16)


def pack(fq, fk, fv):
    return pl.pallas_call(
        pack_kernel,
        out_shape=jax.ShapeDtypeStruct((NHEAD, 16, PACKED), bf16),
        compiler_params=params(16),
    )(fq, fk, fv)


def unpack_kernel(place_ref, lengths_ref, in_ref, q_ref, k_ref, v_ref, bias_ref):
    mask = lower_half((8, GROUP // 2))
    tops = [[], [], []]
    rests = [[], [], []]
    for s in range(NHEAD):
        both = in_ref[s].astype(f32)
        flat = jnp.concatenate([both[0:8], both[8:16]], axis=1)
        for i in range(3):
            tops[i].append(flat[:, i * GROUP:(i + 1) * GROUP])
            base = 3 * GROUP + i * (GROUP // 2)
            rests[i].append(flat[:, base:base + GROUP // 2])
    for i, ref in enumerate((q_ref, k_ref, v_ref)):
        tiles = list(tops[i])
        for k in range(NHEAD // 2):
            a, b = rests[i][2 * k], rests[i][2 * k + 1]
            left = jnp.where(mask, a, pltpu.roll(b, 4, 0))
            right = jnp.where(mask, pltpu.roll(a, 4, 0), b)
            tiles.append(jnp.concatenate([left, right], axis=1))
        ref[...] = jnp.concatenate(tiles, axis=0).astype(bf16)

    z, yh, c = place_ref[0], place_ref[1], place_ref[2]
    row = lax.broadcasted_iota(jnp.int32, (CAP, HD), 0)
    mine = lax.broadcasted_iota(jnp.int32, (CAP, HD), 1) == yh
    for j in range(NZ * NC):
        length = lengths_ref[(j // NC) * NY * NC + yh * NC + j % NC]
        hidden_length = jnp.where((j // NC == z) & (j % NC == c), 0, length)
        seen = row < jnp.where(mine, hidden_length, length)
        bias_ref[j * CAP:(j + 1) * CAP] = jnp.where(seen, 0.0, BIG).astype(bf16)
    rest = row - 64
    token = jnp.where(row < 64, 12 * (row >> 3) + (row & 7), 12 * (rest >> 2) + 8 + (rest & 3))
    own_length = lengths_ref[z * NY * NC + yh * NC + c]
    seen = token < jnp.where(mine, own_length, 0)
    bias_ref[KEYS:] = jnp.where(seen, 0.0, BIG).astype(bf16)


def unpack(place, lengths, received):
    one = jax.ShapeDtypeStruct((CAP, GROUP), bf16)
    smem = pl.BlockSpec(memory_space=pltpu.SMEM)
    vmem = pl.BlockSpec(memory_space=pltpu.VMEM)
    return pl.pallas_call(
        unpack_kernel,
        in_specs=[smem, smem, vmem],
        out_specs=(vmem,) * 4,
        out_shape=(one, one, one, jax.ShapeDtypeStruct((KEYS + CAP, HD), bf16)),
        compiler_params=params(16),
    )(place, lengths, received)


def attention_kernel(q_ref, k_ref, v_ref, kf_ref, vf_ref, hot_ref, bias_ref, out_ref):
    h = pl.program_id(0)
    lane = lax.broadcasted_iota(jnp.int32, (QUERIES, HD), 1)
    query = jnp.concatenate([q_ref[...], hot_ref[...]], axis=1)
    chunk = KEYS // 4
    pieces = [(k_ref[i:i + chunk], v_ref[i:i + chunk], bias_ref[i:i + chunk]) for i in range(0, KEYS, chunk)]
    pieces.append((kf_ref[...], vf_ref[...], bias_ref[KEYS:]))
    scores = []
    for key, _, bias in pieces:
        key = jnp.concatenate([key, bias], axis=1)
        scores.append(lax.dot_general(query, key, (((1,), (1,)), ((), ())), preferred_element_type=f32))
    top = scores[0].max(axis=1, keepdims=True)
    for s in scores[1:]:
        top = jnp.maximum(top, s.max(axis=1, keepdims=True))
    total = jnp.zeros((QUERIES, 1), f32)
    accum = jnp.zeros((QUERIES, HD), f32)
    for s, (_, value, _) in zip(scores, pieces):
        weights = jnp.exp2((s - top) * EXP2_SCALE)
        total = total + weights.sum(axis=1, keepdims=True)
        accum = accum + jnp.dot(weights.astype(bf16), value, preferred_element_type=f32)
    out_ref[:, pl.ds(pl.multiple_of(h * HD, HD), HD)] = (accum / total).astype(bf16)
    level = top * EXP2_SCALE + jnp.log2(total)
    hi = level.astype(bf16).astype(f32)
    mid = (level - hi).astype(bf16).astype(f32)
    low = level - hi - mid
    stat = jnp.where(lane == 3 * h, hi, 0.0)
    stat = jnp.where(lane == 3 * h + 1, mid, stat)
    stat = jnp.where(lane == 3 * h + 2, low, stat).astype(bf16)

    @pl.when(h == 0)
    def _():
        out_ref[:, GROUP:] = stat

    @pl.when(h != 0)
    def _():
        out_ref[:, GROUP:] = out_ref[:, GROUP:] + stat


def attention(q, kv, kf, vf, bias):
    hot = np.zeros((QUERIES, HD), np.float32)
    hot[np.arange(QUERIES), np.arange(QUERIES) // CAP] = 1

    def column(rows, skip=0):
        return pl.BlockSpec((rows, HD), lambda h: (0, h + skip))

    def whole(rows, cols):
        return pl.BlockSpec((rows, cols), lambda h: (0, 0))

    return pl.pallas_call(
        attention_kernel,
        grid=(HEADS_HERE,),
        in_specs=[
            column(QUERIES), column(KEYS), column(KEYS, HEADS_HERE), column(CAP), column(CAP),
            whole(QUERIES, HD), whole(KEYS + CAP, HD),
        ],
        out_specs=whole(QUERIES, GROUP + HD),
        out_shape=jax.ShapeDtypeStruct((QUERIES, GROUP + HD), bf16),
        compiler_params=params(40),
        cost_estimate=pl.CostEstimate(
            flops=4 * QUERIES * (KEYS + CAP) * GROUP,
            bytes_accessed=4 * KEYS * GROUP,
            transcendentals=QUERIES * (KEYS + CAP) * HEADS_HERE,
        ),
    )(q, kv, kv, kf, vf, jnp.asarray(hot, bf16), bias)


def project_kernel(part_ref, w_ref, out_ref, w_vmem, sem):
    copy = pltpu.make_async_copy(w_ref, w_vmem, sem)
    copy.start()
    stats = [part_ref[b, :, GROUP:].astype(f32) for b in range(NY)]
    heads = []
    for h in range(HEADS_HERE):
        levels = [s[:, 3 * h:3 * h + 1] + s[:, 3 * h + 1:3 * h + 2] + s[:, 3 * h + 2:3 * h + 3] for s in stats]
        top = levels[0]
        for level in levels[1:]:
            top = jnp.maximum(top, level)
        total = jnp.zeros((CAP, 1), f32)
        accum = jnp.zeros((CAP, HD), f32)
        for b in range(NY):
            weight = jnp.exp2(levels[b] - top)
            total = total + weight
            accum = accum + weight * part_ref[b, :, h * HD:(h + 1) * HD].astype(f32)
        heads.append((accum / total).astype(bf16))
    attended = jnp.concatenate(heads, axis=1)
    copy.wait()
    half = D // 2
    step = 384
    mask = lower_half((8, step))
    for j in range(half // step):
        left = jnp.dot(attended, w_vmem[:, j * step:(j + 1) * step], preferred_element_type=f32)
        right = jnp.dot(attended, w_vmem[:, half + j * step:half + (j + 1) * step], preferred_element_type=f32)
        for s in range(NHEAD):
            k = s // 2
            a = left[64 + 8 * k:72 + 8 * k]
            b = right[64 + 8 * k:72 + 8 * k]
            if s % 2 == 0:
                rest = jnp.where(mask, a, pltpu.roll(b, 4, 0))
            else:
                rest = jnp.where(mask, pltpu.roll(a, 4, 0), b)
            pieces = (
                (j * step, left[8 * s:8 * s + 8]),
                (half + j * step, right[8 * s:8 * s + 8]),
                (D + j * step, rest),
            )
            for col, tile in pieces:
                row = 8 * (col // OUT_PACKED)
                col = col % OUT_PACKED
                assert col + step <= OUT_PACKED
                out_ref[s, row:row + 8, col:col + step] = tile.astype(bf16)


def project(parts, w):
    return pl.pallas_call(
        project_kernel,
        in_specs=[pl.BlockSpec(memory_space=pltpu.VMEM), pl.BlockSpec(memory_space=pl.ANY)],
        out_specs=pl.BlockSpec(memory_space=pltpu.VMEM),
        out_shape=jax.ShapeDtypeStruct((NHEAD, 16, OUT_PACKED), bf16),
        scratch_shapes=[pltpu.VMEM((GROUP, D), bf16), pltpu.SemaphoreType.DMA],
        compiler_params=params(24),
    )(parts, w)


def mix_kernel(limit_ref, in_ref, hidden_ref, gate_ref, out_ref):
    total = in_ref[0].astype(f32)
    for s in range(1, NHEAD):
        total = total + in_ref[s].astype(f32)
    flat = jnp.concatenate([total[0:8], total[8:16]], axis=1)
    half = D // 2
    rest = flat[:, D:]
    tail = jnp.concatenate([rest[0:4], rest[4:8]], axis=1)
    projected = jnp.concatenate([flat[:, :D], tail], axis=0)
    residual = hidden_ref[...].astype(f32)
    live = lax.broadcasted_iota(jnp.int32, (OWN, D), 0) < limit_ref[0]
    mixed = jnp.where(live, residual + gate_ref[...] * projected, residual)
    out_ref[...] = mixed.astype(bf16)


def mix(limit, received, hidden, gate):
    vmem = pl.BlockSpec(memory_space=pltpu.VMEM)
    return pl.pallas_call(
        mix_kernel,
        in_specs=[pl.BlockSpec(memory_space=pltpu.SMEM), vmem, vmem, vmem],
        out_specs=vmem,
        out_shape=jax.ShapeDtypeStruct((OWN, D), bf16),
        compiler_params=params(16),
    )(limit, received, hidden, gate)


def swap(x, axis):
    return lax.all_to_all(x, axis, split_axis=0, concat_axis=0, tiled=True)


def local(fq, fk, fv, sk, sv, lengths, hidden, gate, w):
    z, yh, c = (lax.axis_index(a) for a in ("z", "yh", "c"))
    own_head = lax.axis_index("yl") * NX + lax.axis_index("x")

    place = jnp.stack([z, yh, c]).astype(jnp.int32)
    kv = lax.all_gather(jnp.concatenate([sk, sv], axis=1), ("z", "c"), axis=0, tiled=True)
    query, kf, vf, bias = unpack(place, lengths, swap(pack(fq, fk, fv), HEAD))
    queries = lax.all_gather(query, "yh", axis=0, tiled=True)
    parts = attention(queries, kv, kf, vf, bias)
    parts = swap(parts.reshape(NY, CAP, GROUP + HD), "yh")
    packed = project(parts, w)
    own_length = lax.dynamic_index_in_dim(lengths, (z * NY + yh) * NC + c, 0, keepdims=False)
    limit = jnp.clip(own_length - own_head * OWN, 0, OWN)[None]
    return mix(limit, swap(packed, HEAD), hidden, gate[None, :])


def solution(mesh):
    grid = Mesh(mesh.devices.reshape(NZ, NY, NC, NYL, NX), ALL)
    rows = P(ALL, None)
    stale = P(("z", "yh", "c"), HEAD)
    in_specs = (rows, rows, rows, stale, stale, P(), rows, P(), P(HEAD, None))
    return jax.shard_map(local, mesh=grid, in_specs=in_specs, out_specs=rows, check_vma=False)
```

```python
import jax
import jax.numpy as jnp
import numpy as np
from jax import lax
from jax.experimental import pallas as pl
from jax.experimental.pallas import tpu as pltpu
from jax.sharding import Mesh, PartitionSpec as P

HD = 128
CAP = 96
NZ, NY, NC, NYL, NX = 8, 4, 2, 2, 4
NHEAD = NYL * NX
GROUP = 512
HEADS_HERE = GROUP // HD
OWN = 12
D = 3072
KEYS = NZ * NC * CAP
QUERIES = NY * CAP
BIG = -1e30
TOGETHER = 2
EXP2_SCALE = float(np.log2(np.e) * HD ** (-0.5))
HEAD = ("yl", "x")
ALL = ("z", "yh", "c", "yl", "x")
f32 = jnp.float32
bf16 = jnp.bfloat16
PACKED = 3 * 768 // 2
OUT_PACKED = (D + D // 2) // 2


def params(mb):
    return pltpu.CompilerParams(vmem_limit_bytes=mb * 2**20)


def lower_half(shape):
    return lax.broadcasted_iota(jnp.int32, shape, 0) < 4


def pack_kernel(q_ref, k_ref, v_ref, out_ref):
    mask = lower_half((8, GROUP // 2))
    for h in range(NHEAD):
        tops, rests = [], []
        for ref in (q_ref, k_ref, v_ref):
            rows = ref[:, h * GROUP:(h + 1) * GROUP].astype(f32)
            tops.append(rows[0:8])
            tail = rows[4:12]
            first = pltpu.roll(tail[:, : GROUP // 2], 4, 0)
            rests.append(jnp.where(mask, first, tail[:, GROUP // 2:]))
        flat = jnp.concatenate(tops + rests, axis=1)
        both = jnp.concatenate([flat[:, :PACKED], flat[:, PACKED:]], axis=0)
        out_ref[h] = both.astype(bf16)


def pack(fq, fk, fv):
    return pl.pallas_call(
        pack_kernel,
        out_shape=jax.ShapeDtypeStruct((NHEAD, 16, PACKED), bf16),
        compiler_params=params(60),
    )(fq, fk, fv)


def unpack_kernel(place_ref, lengths_ref, in_ref, q_ref, k_ref, v_ref, bias_ref):
    mask = lower_half((8, GROUP // 2))
    tops = [[], [], []]
    rests = [[], [], []]
    for s in range(NHEAD):
        both = in_ref[s].astype(f32)
        flat = jnp.concatenate([both[0:8], both[8:16]], axis=1)
        for i in range(3):
            tops[i].append(flat[:, i * GROUP:(i + 1) * GROUP])
            base = 3 * GROUP + i * (GROUP // 2)
            rests[i].append(flat[:, base:base + GROUP // 2])
    for i, ref in enumerate((q_ref, k_ref, v_ref)):
        tiles = list(tops[i])
        for k in range(NHEAD // 2):
            a, b = rests[i][2 * k], rests[i][2 * k + 1]
            left = jnp.where(mask, a, pltpu.roll(b, 4, 0))
            right = jnp.where(mask, pltpu.roll(a, 4, 0), b)
            tiles.append(jnp.concatenate([left, right], axis=1))
        ref[...] = jnp.concatenate(tiles, axis=0).astype(bf16)

    z, yh, c = place_ref[0], place_ref[1], place_ref[2]
    row = lax.broadcasted_iota(jnp.int32, (CAP, HD), 0)
    mine = lax.broadcasted_iota(jnp.int32, (CAP, HD), 1) == yh
    for j in range(NZ * NC):
        length = lengths_ref[(j // NC) * NY * NC + yh * NC + j % NC]
        hidden_length = jnp.where((j // NC == z) & (j % NC == c), 0, length)
        seen = row < jnp.where(mine, hidden_length, length)
        bias_ref[j * CAP:(j + 1) * CAP] = jnp.where(seen, 0.0, BIG).astype(bf16)
    rest = row - 64
    token = jnp.where(row < 64, 12 * (row >> 3) + (row & 7), 12 * (rest >> 2) + 8 + (rest & 3))
    own_length = lengths_ref[z * NY * NC + yh * NC + c]
    seen = token < jnp.where(mine, own_length, 0)
    bias_ref[KEYS:] = jnp.where(seen, 0.0, BIG).astype(bf16)


def unpack(place, lengths, received):
    one = jax.ShapeDtypeStruct((CAP, GROUP), bf16)
    smem = pl.BlockSpec(memory_space=pltpu.SMEM)
    vmem = pl.BlockSpec(memory_space=pltpu.VMEM)
    return pl.pallas_call(
        unpack_kernel,
        in_specs=[smem, smem, vmem],
        out_specs=(vmem,) * 4,
        out_shape=(one, one, one, jax.ShapeDtypeStruct((KEYS + CAP, HD), bf16)),
        compiler_params=params(16),
    )(place, lengths, received)


def attention_kernel(q_ref, k_ref, v_ref, kf_ref, vf_ref, hot_ref, bias_ref, out_ref):
    g = pl.program_id(0)
    lane = lax.broadcasted_iota(jnp.int32, (QUERIES, HD), 1)
    stat = jnp.zeros((QUERIES, HD), f32)
    chunk = KEYS // 4
    for i in range(TOGETHER):
        cols = slice(i * HD, (i + 1) * HD)
        query = jnp.concatenate([q_ref[:, cols], hot_ref[...]], axis=1)
        pieces = [
            (k_ref[j:j + chunk, cols], v_ref[j:j + chunk, cols], bias_ref[j:j + chunk])
            for j in range(0, KEYS, chunk)
        ]
        pieces.append((kf_ref[:, cols], vf_ref[:, cols], bias_ref[KEYS:]))
        scores = []
        for key, _, bias in pieces:
            key = jnp.concatenate([key, bias], axis=1)
            scores.append(lax.dot_general(query, key, (((1,), (1,)), ((), ())), preferred_element_type=f32))
        top = scores[0].max(axis=1, keepdims=True)
        for s in scores[1:]:
            top = jnp.maximum(top, s.max(axis=1, keepdims=True))
        total = jnp.zeros((QUERIES, 1), f32)
        accum = jnp.zeros((QUERIES, HD), f32)
        for s, (_, value, _) in zip(scores, pieces):
            weights = jnp.exp2((s - top) * EXP2_SCALE)
            total = total + weights.sum(axis=1, keepdims=True)
            accum = accum + jnp.dot(weights.astype(bf16), value, preferred_element_type=f32)
        h = g * TOGETHER + i
        out_ref[:, pl.ds(pl.multiple_of(h * HD, HD), HD)] = (accum / total).astype(bf16)
        level = top * EXP2_SCALE + jnp.log2(total)
        hi = level.astype(bf16).astype(f32)
        mid = (level - hi).astype(bf16).astype(f32)
        low = level - hi - mid
        stat = jnp.where(lane == 3 * h, hi, stat)
        stat = jnp.where(lane == 3 * h + 1, mid, stat)
        stat = jnp.where(lane == 3 * h + 2, low, stat)
    stat = stat.astype(bf16)

    @pl.when(g == 0)
    def _():
        out_ref[:, GROUP:] = stat

    @pl.when(g != 0)
    def _():
        out_ref[:, GROUP:] = out_ref[:, GROUP:] + stat


def attention(q, kv, kf, vf, bias):
    hot = np.zeros((QUERIES, HD), np.float32)
    hot[np.arange(QUERIES), np.arange(QUERIES) // CAP] = 1
    steps = HEADS_HERE // TOGETHER

    def column(rows, skip=0):
        return pl.BlockSpec((rows, TOGETHER * HD), lambda g: (0, g + skip))

    def whole(rows, cols):
        return pl.BlockSpec((rows, cols), lambda g: (0, 0))

    return pl.pallas_call(
        attention_kernel,
        grid=(steps,),
        in_specs=[
            column(QUERIES), column(KEYS), column(KEYS, steps), column(CAP), column(CAP),
            whole(QUERIES, HD), whole(KEYS + CAP, HD),
        ],
        out_specs=whole(QUERIES, GROUP + HD),
        out_shape=jax.ShapeDtypeStruct((QUERIES, GROUP + HD), bf16),
        compiler_params=params(60),
        cost_estimate=pl.CostEstimate(
            flops=4 * QUERIES * (KEYS + CAP) * GROUP,
            bytes_accessed=4 * KEYS * GROUP,
            transcendentals=QUERIES * (KEYS + CAP) * HEADS_HERE,
        ),
    )(q, kv, kv, kf, vf, jnp.asarray(hot, bf16), bias)


def project_kernel(part_ref, w_ref, out_ref):
    stats = [part_ref[b, :, GROUP:].astype(f32) for b in range(NY)]
    heads = []
    for h in range(HEADS_HERE):
        levels = [s[:, 3 * h:3 * h + 1] + s[:, 3 * h + 1:3 * h + 2] + s[:, 3 * h + 2:3 * h + 3] for s in stats]
        top = levels[0]
        for level in levels[1:]:
            top = jnp.maximum(top, level)
        total = jnp.zeros((CAP, 1), f32)
        accum = jnp.zeros((CAP, HD), f32)
        for b in range(NY):
            weight = jnp.exp2(levels[b] - top)
            total = total + weight
            accum = accum + weight * part_ref[b, :, h * HD:(h + 1) * HD].astype(f32)
        heads.append((accum / total).astype(bf16))
    attended = jnp.concatenate(heads, axis=1)
    half = D // 2
    step = 384
    mask = lower_half((8, step))
    for j in range(half // step):
        left = jnp.dot(attended, w_ref[:, j * step:(j + 1) * step], preferred_element_type=f32)
        right = jnp.dot(attended, w_ref[:, half + j * step:half + (j + 1) * step], preferred_element_type=f32)
        for s in range(NHEAD):
            k = s // 2
            a = left[64 + 8 * k:72 + 8 * k]
            b = right[64 + 8 * k:72 + 8 * k]
            if s % 2 == 0:
                rest = jnp.where(mask, a, pltpu.roll(b, 4, 0))
            else:
                rest = jnp.where(mask, pltpu.roll(a, 4, 0), b)
            pieces = (
                (j * step, left[8 * s:8 * s + 8]),
                (half + j * step, right[8 * s:8 * s + 8]),
                (D + j * step, rest),
            )
            for col, tile in pieces:
                row = 8 * (col // OUT_PACKED)
                col = col % OUT_PACKED
                assert col + step <= OUT_PACKED
                out_ref[s, row:row + 8, col:col + step] = tile.astype(bf16)


def project(parts, w):
    return pl.pallas_call(
        project_kernel,
        in_specs=[pl.BlockSpec(memory_space=pltpu.VMEM)] * 2,
        out_specs=pl.BlockSpec(memory_space=pltpu.VMEM),
        out_shape=jax.ShapeDtypeStruct((NHEAD, 16, OUT_PACKED), bf16),
        compiler_params=params(24),
    )(parts, w)


def mix_kernel(limit_ref, in_ref, hidden_ref, gate_ref, out_ref):
    total = in_ref[0].astype(f32)
    for s in range(1, NHEAD):
        total = total + in_ref[s].astype(f32)
    flat = jnp.concatenate([total[0:8], total[8:16]], axis=1)
    half = D // 2
    rest = flat[:, D:]
    tail = jnp.concatenate([rest[0:4], rest[4:8]], axis=1)
    projected = jnp.concatenate([flat[:, :D], tail], axis=0)
    residual = hidden_ref[...].astype(f32)
    live = lax.broadcasted_iota(jnp.int32, (OWN, D), 0) < limit_ref[0]
    mixed = jnp.where(live, residual + gate_ref[...] * projected, residual)
    out_ref[...] = mixed.astype(bf16)


def mix(limit, received, hidden, gate):
    vmem = pl.BlockSpec(memory_space=pltpu.VMEM)
    return pl.pallas_call(
        mix_kernel,
        in_specs=[pl.BlockSpec(memory_space=pltpu.SMEM), vmem, vmem, vmem],
        out_specs=vmem,
        out_shape=jax.ShapeDtypeStruct((OWN, D), bf16),
        compiler_params=params(16),
    )(limit, received, hidden, gate)


def swap(x, axis):
    return lax.all_to_all(x, axis, split_axis=0, concat_axis=0, tiled=True)


def local(fq, fk, fv, sk, sv, lengths, hidden, gate, w):
    z, yh, c = (lax.axis_index(a) for a in ("z", "yh", "c"))
    own_head = lax.axis_index("yl") * NX + lax.axis_index("x")

    place = jnp.stack([z, yh, c]).astype(jnp.int32)
    kv = lax.all_gather(jnp.concatenate([sk, sv], axis=1), ("z", "c"), axis=0, tiled=True)
    query, kf, vf, bias = unpack(place, lengths, swap(pack(fq, fk, fv), HEAD))
    queries = lax.all_gather(query, "yh", axis=0, tiled=True)
    parts = attention(queries, kv, kf, vf, bias)
    parts = swap(parts.reshape(NY, CAP, GROUP + HD), "yh")
    packed = project(parts, w)
    own_length = lax.dynamic_index_in_dim(lengths, (z * NY + yh) * NC + c, 0, keepdims=False)
    limit = jnp.clip(own_length - own_head * OWN, 0, OWN)[None]
    return mix(limit, swap(packed, HEAD), hidden, gate[None, :])


def solution(mesh):
    grid = Mesh(mesh.devices.reshape(NZ, NY, NC, NYL, NX), ALL)
    rows = P(ALL, None)
    stale = P(("z", "yh", "c"), HEAD)
    in_specs = (rows, rows, rows, stale, stale, P(), rows, P(), P(HEAD, None))
    return jax.shard_map(local, mesh=grid, in_specs=in_specs, out_specs=rows, check_vma=False)
```

```python
import jax
import jax.numpy as jnp
import numpy as np
from jax import lax
from jax.experimental import pallas as pl
from jax.experimental.pallas import tpu as pltpu
from jax.sharding import Mesh, PartitionSpec as P

HD = 128
CAP = 96
NZ, NY, NC, NYL, NX = 8, 4, 2, 2, 4
NHEAD = NYL * NX
GROUP = 512
HEADS_HERE = GROUP // HD
OWN = 12
D = 3072
KEYS = NZ * NC * CAP
QUERIES = NY * CAP
BIG = -1e30
TOGETHER = 2
STAT_ROWS = 16
RETURNED = HEADS_HERE * CAP + STAT_ROWS
EXP2_SCALE = float(np.log2(np.e) * HD ** (-0.5))
HEAD = ("yl", "x")
ALL = ("z", "yh", "c", "yl", "x")
f32 = jnp.float32
bf16 = jnp.bfloat16
PACKED = 3 * 768 // 2
OUT_PACKED = (D + D // 2) // 2


def params(mb):
    return pltpu.CompilerParams(vmem_limit_bytes=mb * 2**20)


def lower_half(shape):
    return lax.broadcasted_iota(jnp.int32, shape, 0) < 4


def pack_kernel(q_ref, k_ref, v_ref, out_ref):
    mask = lower_half((8, GROUP // 2))
    for h in range(NHEAD):
        tops, rests = [], []
        for ref in (q_ref, k_ref, v_ref):
            rows = ref[:, h * GROUP:(h + 1) * GROUP].astype(f32)
            tops.append(rows[0:8])
            tail = rows[4:12]
            first = pltpu.roll(tail[:, : GROUP // 2], 4, 0)
            rests.append(jnp.where(mask, first, tail[:, GROUP // 2:]))
        flat = jnp.concatenate(tops + rests, axis=1)
        both = jnp.concatenate([flat[:, :PACKED], flat[:, PACKED:]], axis=0)
        out_ref[h] = both.astype(bf16)


def pack(fq, fk, fv):
    return pl.pallas_call(
        pack_kernel,
        out_shape=jax.ShapeDtypeStruct((NHEAD, 16, PACKED), bf16),
        compiler_params=params(60),
    )(fq, fk, fv)


def unpack_kernel(place_ref, lengths_ref, in_ref, q_ref, k_ref, v_ref, bias_ref):
    mask = lower_half((8, GROUP // 2))
    tops = [[], [], []]
    rests = [[], [], []]
    for s in range(NHEAD):
        both = in_ref[s].astype(f32)
        flat = jnp.concatenate([both[0:8], both[8:16]], axis=1)
        for i in range(3):
            tops[i].append(flat[:, i * GROUP:(i + 1) * GROUP])
            base = 3 * GROUP + i * (GROUP // 2)
            rests[i].append(flat[:, base:base + GROUP // 2])
    for i, ref in enumerate((q_ref, k_ref, v_ref)):
        tiles = list(tops[i])
        for k in range(NHEAD // 2):
            a, b = rests[i][2 * k], rests[i][2 * k + 1]
            left = jnp.where(mask, a, pltpu.roll(b, 4, 0))
            right = jnp.where(mask, pltpu.roll(a, 4, 0), b)
            tiles.append(jnp.concatenate([left, right], axis=1))
        ref[...] = jnp.concatenate(tiles, axis=0).astype(bf16)

    z, yh, c = place_ref[0], place_ref[1], place_ref[2]
    row = lax.broadcasted_iota(jnp.int32, (CAP, HD), 0)
    mine = lax.broadcasted_iota(jnp.int32, (CAP, HD), 1) == yh
    for j in range(NZ * NC):
        length = lengths_ref[(j // NC) * NY * NC + yh * NC + j % NC]
        hidden_length = jnp.where((j // NC == z) & (j % NC == c), 0, length)
        seen = row < jnp.where(mine, hidden_length, length)
        bias_ref[j * CAP:(j + 1) * CAP] = jnp.where(seen, 0.0, BIG).astype(bf16)
    rest = row - 64
    token = jnp.where(row < 64, 12 * (row >> 3) + (row & 7), 12 * (rest >> 2) + 8 + (rest & 3))
    own_length = lengths_ref[z * NY * NC + yh * NC + c]
    seen = token < jnp.where(mine, own_length, 0)
    bias_ref[KEYS:] = jnp.where(seen, 0.0, BIG).astype(bf16)


def unpack(place, lengths, received):
    one = jax.ShapeDtypeStruct((CAP, GROUP), bf16)
    smem = pl.BlockSpec(memory_space=pltpu.SMEM)
    vmem = pl.BlockSpec(memory_space=pltpu.VMEM)
    return pl.pallas_call(
        unpack_kernel,
        in_specs=[smem, smem, vmem],
        out_specs=(vmem,) * 4,
        out_shape=(one, one, one, jax.ShapeDtypeStruct((KEYS + CAP, HD), bf16)),
        compiler_params=params(16),
    )(place, lengths, received)


def attention_kernel(q_ref, k_ref, v_ref, kf_ref, vf_ref, hot_ref, bias_ref, out_ref, stat_ref):
    g = pl.program_id(0)
    lane = lax.broadcasted_iota(jnp.int32, (QUERIES, HD), 1)
    stat = jnp.zeros((QUERIES, HD), f32)
    chunk = KEYS // 4
    for i in range(TOGETHER):
        cols = slice(i * HD, (i + 1) * HD)
        query = jnp.concatenate([q_ref[:, cols], hot_ref[...]], axis=1)
        pieces = [
            (k_ref[j:j + chunk, cols], v_ref[j:j + chunk, cols], bias_ref[j:j + chunk])
            for j in range(0, KEYS, chunk)
        ]
        pieces.append((kf_ref[:, cols], vf_ref[:, cols], bias_ref[KEYS:]))
        scores = []
        for key, _, bias in pieces:
            key = jnp.concatenate([key, bias], axis=1)
            scores.append(lax.dot_general(query, key, (((1,), (1,)), ((), ())), preferred_element_type=f32))
        top = scores[0].max(axis=1, keepdims=True)
        for s in scores[1:]:
            top = jnp.maximum(top, s.max(axis=1, keepdims=True))
        total = jnp.zeros((QUERIES, 1), f32)
        accum = jnp.zeros((QUERIES, HD), f32)
        for s, (_, value, _) in zip(scores, pieces):
            weights = jnp.exp2((s - top) * EXP2_SCALE)
            total = total + weights.sum(axis=1, keepdims=True)
            accum = accum + jnp.dot(weights.astype(bf16), value, preferred_element_type=f32)
        h = g * TOGETHER + i
        result = (accum / total).astype(bf16)
        for b in range(NY):
            out_ref[b, pl.ds(pl.multiple_of(h * CAP, 32), CAP), :] = result[b * CAP:(b + 1) * CAP]
        level = top * EXP2_SCALE + jnp.log2(total)
        hi = level.astype(bf16).astype(f32)
        mid = (level - hi).astype(bf16).astype(f32)
        low = level - hi - mid
        stat = jnp.where(lane == 3 * h, hi, stat)
        stat = jnp.where(lane == 3 * h + 1, mid, stat)
        stat = jnp.where(lane == 3 * h + 2, low, stat)

    @pl.when(g == 0)
    def _():
        stat_ref[...] = stat

    @pl.when(g != 0)
    def _():
        stat_ref[...] = stat_ref[...] + stat

    @pl.when(g == pl.num_programs(0) - 1)
    def _():
        for b in range(NY):
            rows = stat_ref[b * CAP:(b + 1) * CAP]
            square = jnp.concatenate([rows, jnp.zeros((HD - CAP, HD), f32)], axis=0)
            out_ref[b, HEADS_HERE * CAP:, :] = square.T[:STAT_ROWS].astype(bf16)


def attention(q, kv, kf, vf, bias):
    hot = np.zeros((QUERIES, HD), np.float32)
    hot[np.arange(QUERIES), np.arange(QUERIES) // CAP] = 1
    steps = HEADS_HERE // TOGETHER

    def column(rows, skip=0):
        return pl.BlockSpec((rows, TOGETHER * HD), lambda g: (0, g + skip))

    def whole(rows, cols):
        return pl.BlockSpec((rows, cols), lambda g: (0, 0))

    return pl.pallas_call(
        attention_kernel,
        grid=(steps,),
        in_specs=[
            column(QUERIES), column(KEYS), column(KEYS, steps), column(CAP), column(CAP),
            whole(QUERIES, HD), whole(KEYS + CAP, HD),
        ],
        out_specs=pl.BlockSpec((NY, RETURNED, HD), lambda g: (0, 0, 0)),
        out_shape=jax.ShapeDtypeStruct((NY, RETURNED, HD), bf16),
        scratch_shapes=[pltpu.VMEM((QUERIES, HD), f32)],
        compiler_params=params(60),
        cost_estimate=pl.CostEstimate(
            flops=4 * QUERIES * (KEYS + CAP) * GROUP,
            bytes_accessed=4 * KEYS * GROUP,
            transcendentals=QUERIES * (KEYS + CAP) * HEADS_HERE,
        ),
    )(q, kv, kv, kf, vf, jnp.asarray(hot, bf16), bias)


def project_kernel(part_ref, w_ref, out_ref):
    stats = [part_ref[b, HEADS_HERE * CAP:, :].astype(f32) for b in range(NY)]
    shares = []
    for h in range(HEADS_HERE):
        levels = [s[3 * h:3 * h + 1] + s[3 * h + 1:3 * h + 2] + s[3 * h + 2:3 * h + 3] for s in stats]
        top = levels[0]
        for level in levels[1:]:
            top = jnp.maximum(top, level)
        weights = [jnp.exp2(level - top) for level in levels]
        total = weights[0]
        for weight in weights[1:]:
            total = total + weight
        shares += [weight / total for weight in weights]
    shares = jnp.concatenate(shares + [jnp.zeros((HD - len(shares), HD), f32)], axis=0).T
    heads = []
    for h in range(HEADS_HERE):
        accum = jnp.zeros((CAP, HD), f32)
        for b in range(NY):
            share = shares[:CAP, h * NY + b:h * NY + b + 1]
            accum = accum + share * part_ref[b, h * CAP:(h + 1) * CAP, :].astype(f32)
        heads.append(accum.astype(bf16))
    attended = jnp.concatenate(heads, axis=1)
    half = D // 2
    step = 384
    mask = lower_half((8, step))
    for j in range(half // step):
        left = jnp.dot(attended, w_ref[:, j * step:(j + 1) * step], preferred_element_type=f32)
        right = jnp.dot(attended, w_ref[:, half + j * step:half + (j + 1) * step], preferred_element_type=f32)
        for s in range(NHEAD):
            k = s // 2
            a = left[64 + 8 * k:72 + 8 * k]
            b = right[64 + 8 * k:72 + 8 * k]
            if s % 2 == 0:
                rest = jnp.where(mask, a, pltpu.roll(b, 4, 0))
            else:
                rest = jnp.where(mask, pltpu.roll(a, 4, 0), b)
            pieces = (
                (j * step, left[8 * s:8 * s + 8]),
                (half + j * step, right[8 * s:8 * s + 8]),
                (D + j * step, rest),
            )
            for col, tile in pieces:
                row = 8 * (col // OUT_PACKED)
                col = col % OUT_PACKED
                assert col + step <= OUT_PACKED
                out_ref[s, row:row + 8, col:col + step] = tile.astype(bf16)


def project(parts, w):
    return pl.pallas_call(
        project_kernel,
        in_specs=[pl.BlockSpec(memory_space=pltpu.VMEM)] * 2,
        out_specs=pl.BlockSpec(memory_space=pltpu.VMEM),
        out_shape=jax.ShapeDtypeStruct((NHEAD, 16, OUT_PACKED), bf16),
        compiler_params=params(24),
    )(parts, w)


def mix_kernel(limit_ref, in_ref, hidden_ref, gate_ref, out_ref):
    total = in_ref[0].astype(f32)
    for s in range(1, NHEAD):
        total = total + in_ref[s].astype(f32)
    flat = jnp.concatenate([total[0:8], total[8:16]], axis=1)
    half = D // 2
    rest = flat[:, D:]
    tail = jnp.concatenate([rest[0:4], rest[4:8]], axis=1)
    projected = jnp.concatenate([flat[:, :D], tail], axis=0)
    residual = hidden_ref[...].astype(f32)
    live = lax.broadcasted_iota(jnp.int32, (OWN, D), 0) < limit_ref[0]
    mixed = jnp.where(live, residual + gate_ref[...] * projected, residual)
    out_ref[...] = mixed.astype(bf16)


def mix(limit, received, hidden, gate):
    vmem = pl.BlockSpec(memory_space=pltpu.VMEM)
    return pl.pallas_call(
        mix_kernel,
        in_specs=[pl.BlockSpec(memory_space=pltpu.SMEM), vmem, vmem, vmem],
        out_specs=vmem,
        out_shape=jax.ShapeDtypeStruct((OWN, D), bf16),
        compiler_params=params(16),
    )(limit, received, hidden, gate)


def swap(x, axis):
    return lax.all_to_all(x, axis, split_axis=0, concat_axis=0, tiled=True)


def local(fq, fk, fv, sk, sv, lengths, hidden, gate, w):
    z, yh, c = (lax.axis_index(a) for a in ("z", "yh", "c"))
    own_head = lax.axis_index("yl") * NX + lax.axis_index("x")

    place = jnp.stack([z, yh, c]).astype(jnp.int32)
    kv = lax.all_gather(jnp.concatenate([sk, sv], axis=1), ("z", "c"), axis=0, tiled=True)
    query, kf, vf, bias = unpack(place, lengths, swap(pack(fq, fk, fv), HEAD))
    queries = lax.all_gather(query, "yh", axis=0, tiled=True)
    parts = attention(queries, kv, kf, vf, bias)
    packed = project(swap(parts, "yh"), w)
    own_length = lax.dynamic_index_in_dim(lengths, (z * NY + yh) * NC + c, 0, keepdims=False)
    limit = jnp.clip(own_length - own_head * OWN, 0, OWN)[None]
    return mix(limit, swap(packed, HEAD), hidden, gate[None, :])


def solution(mesh):
    grid = Mesh(mesh.devices.reshape(NZ, NY, NC, NYL, NX), ALL)
    rows = P(ALL, None)
    stale = P(("z", "yh", "c"), HEAD)
    in_specs = (rows, rows, rows, stale, stale, P(), rows, P(), P(HEAD, None))
    return jax.shard_map(local, mesh=grid, in_specs=in_specs, out_specs=rows, check_vma=False)
```

```python
import jax
import jax.numpy as jnp
import numpy as np
from jax import lax
from jax.experimental import pallas as pl
from jax.experimental.pallas import tpu as pltpu
from jax.sharding import Mesh, PartitionSpec as P

HD = 128
CAP = 96
NZ, NY, NC, NYL, NX = 8, 4, 2, 2, 4
NHEAD = NYL * NX
GROUP = 512
HEADS_HERE = GROUP // HD
OWN = 12
D = 3072
KEYS = NZ * NC * CAP
QUERIES = NY * CAP
BIG = -1e30
TOGETHER = 2
STAT_ROWS = 16
RETURNED = HEADS_HERE * CAP + STAT_ROWS
EXP2_SCALE = float(np.log2(np.e) * HD ** (-0.5))
HEAD = ("yl", "x")
ALL = ("z", "yh", "c", "yl", "x")
f32 = jnp.float32
bf16 = jnp.bfloat16
PACKED = 3 * 768 // 2
OUT_PACKED = (D + D // 2) // 2


def params(mb):
    return pltpu.CompilerParams(vmem_limit_bytes=mb * 2**20)


def lower_half(shape):
    return lax.broadcasted_iota(jnp.int32, shape, 0) < 4


def pack_kernel(q_ref, k_ref, v_ref, out_ref):
    mask = lower_half((8, GROUP // 2))
    for h in range(NHEAD):
        tops, rests = [], []
        for ref in (q_ref, k_ref, v_ref):
            rows = ref[:, h * GROUP:(h + 1) * GROUP].astype(f32)
            tops.append(rows[0:8])
            tail = rows[4:12]
            first = pltpu.roll(tail[:, : GROUP // 2], 4, 0)
            rests.append(jnp.where(mask, first, tail[:, GROUP // 2:]))
        flat = jnp.concatenate(tops + rests, axis=1)
        both = jnp.concatenate([flat[:, :PACKED], flat[:, PACKED:]], axis=0)
        out_ref[h] = both.astype(bf16)


def pack(fq, fk, fv):
    return pl.pallas_call(
        pack_kernel,
        out_shape=jax.ShapeDtypeStruct((NHEAD, 16, PACKED), bf16),
        compiler_params=params(60),
    )(fq, fk, fv)


def unpack_kernel(place_ref, lengths_ref, in_ref, q_ref, k_ref, v_ref, bias_ref):
    mask = lower_half((8, GROUP // 2))
    tops = [[], [], []]
    rests = [[], [], []]
    for s in range(NHEAD):
        both = in_ref[s].astype(f32)
        flat = jnp.concatenate([both[0:8], both[8:16]], axis=1)
        for i in range(3):
            tops[i].append(flat[:, i * GROUP:(i + 1) * GROUP])
            base = 3 * GROUP + i * (GROUP // 2)
            rests[i].append(flat[:, base:base + GROUP // 2])
    for i, ref in enumerate((q_ref, k_ref, v_ref)):
        tiles = list(tops[i])
        for k in range(NHEAD // 2):
            a, b = rests[i][2 * k], rests[i][2 * k + 1]
            left = jnp.where(mask, a, pltpu.roll(b, 4, 0))
            right = jnp.where(mask, pltpu.roll(a, 4, 0), b)
            tiles.append(jnp.concatenate([left, right], axis=1))
        ref[...] = jnp.concatenate(tiles, axis=0).astype(bf16)

    z, yh, c = place_ref[0], place_ref[1], place_ref[2]
    row = lax.broadcasted_iota(jnp.int32, (CAP, HD), 0)
    mine = lax.broadcasted_iota(jnp.int32, (CAP, HD), 1) == 1
    for j in range(NZ * NC):
        length = lengths_ref[(j // NC) * NY * NC + yh * NC + j % NC]
        hidden_length = jnp.where((j // NC == z) & (j % NC == c), 0, length)
        seen = row < jnp.where(mine, hidden_length, length)
        bias_ref[j * CAP:(j + 1) * CAP] = jnp.where(seen, 0.0, BIG).astype(bf16)
    rest = row - 64
    token = jnp.where(row < 64, 12 * (row >> 3) + (row & 7), 12 * (rest >> 2) + 8 + (rest & 3))
    own_length = lengths_ref[z * NY * NC + yh * NC + c]
    seen = token < jnp.where(mine, own_length, 0)
    bias_ref[KEYS:] = jnp.where(seen, 0.0, BIG).astype(bf16)


def unpack(place, lengths, received):
    one = jax.ShapeDtypeStruct((CAP, GROUP), bf16)
    smem = pl.BlockSpec(memory_space=pltpu.SMEM)
    vmem = pl.BlockSpec(memory_space=pltpu.VMEM)
    return pl.pallas_call(
        unpack_kernel,
        in_specs=[smem, smem, vmem],
        out_specs=(vmem,) * 4,
        out_shape=(one, one, one, jax.ShapeDtypeStruct((KEYS + CAP, HD), bf16)),
        compiler_params=params(16),
    )(place, lengths, received)


def attend(load_query, keys, hot_lane, count):
    rows = count * CAP
    hot = (lax.broadcasted_iota(jnp.int32, (rows, HD), 1) == hot_lane).astype(f32).astype(bf16)
    query = jnp.concatenate([load_query, hot], axis=1)
    scores = []
    for key, _, bias in keys:
        key = jnp.concatenate([key, bias], axis=1)
        scores.append(lax.dot_general(query, key, (((1,), (1,)), ((), ())), preferred_element_type=f32))
    top = scores[0].max(axis=1, keepdims=True)
    for s in scores[1:]:
        top = jnp.maximum(top, s.max(axis=1, keepdims=True))
    total = jnp.zeros((rows, 1), f32)
    accum = jnp.zeros((rows, HD), f32)
    for s, (_, value, _) in zip(scores, keys):
        weights = jnp.exp2((s - top) * EXP2_SCALE)
        total = total + weights.sum(axis=1, keepdims=True)
        accum = accum + jnp.dot(weights.astype(bf16), value, preferred_element_type=f32)
    return (accum / total).astype(bf16), top * EXP2_SCALE + jnp.log2(total)


def add_stat(stat, level, h):
    lane = lax.broadcasted_iota(jnp.int32, stat.shape, 1)
    hi = level.astype(bf16).astype(f32)
    mid = (level - hi).astype(bf16).astype(f32)
    low = level - hi - mid
    stat = jnp.where(lane == 3 * h, hi, stat)
    stat = jnp.where(lane == 3 * h + 1, mid, stat)
    return jnp.where(lane == 3 * h + 2, low, stat)


def stale_pieces(k_ref, v_ref, bias_ref, cols):
    chunk = KEYS // 4
    return [
        (k_ref[j:j + chunk, cols], v_ref[j:j + chunk, cols], bias_ref[j:j + chunk])
        for j in range(0, KEYS, chunk)
    ]


def stat_rows(stat):
    square = jnp.concatenate([stat, jnp.zeros((HD - CAP, HD), f32)], axis=0)
    return square.T[:STAT_ROWS].astype(bf16)


def collect(stat_ref, stat, finish):
    g = pl.program_id(0)

    @pl.when(g == 0)
    def _():
        stat_ref[...] = stat

    @pl.when(g != 0)
    def _():
        stat_ref[...] = stat_ref[...] + stat

    pl.when(g == pl.num_programs(0) - 1)(finish)


def others_kernel(place_ref, q_ref, k_ref, v_ref, bias_ref, out_ref, stat_ref):
    g = pl.program_id(0)
    yh = place_ref[1]
    count = NY - 1
    slots = [lax.rem(yh + k, NY) for k in range(1, NY)]
    stat = jnp.zeros((count * CAP, HD), f32)

    @pl.when(g == 0)
    def _():
        out_ref[yh] = jnp.zeros((RETURNED, HD), bf16)

    for i in range(TOGETHER):
        cols = slice(i * HD, (i + 1) * HD)
        query = jnp.concatenate([q_ref[slot, :, cols] for slot in slots], axis=0)
        result, level = attend(query, stale_pieces(k_ref, v_ref, bias_ref, cols), 0, count)
        h = g * TOGETHER + i
        for n, slot in enumerate(slots):
            out_ref[slot, pl.ds(pl.multiple_of(h * CAP, 32), CAP), :] = result[n * CAP:(n + 1) * CAP]
        stat = add_stat(stat, level, h)

    def finish():
        for n, slot in enumerate(slots):
            out_ref[slot, HEADS_HERE * CAP:, :] = stat_rows(stat_ref[n * CAP:(n + 1) * CAP])

    collect(stat_ref, stat, finish)


def own_kernel(q_ref, k_ref, v_ref, kf_ref, vf_ref, bias_ref, out_ref, stat_ref):
    g = pl.program_id(0)
    stat = jnp.zeros((CAP, HD), f32)
    for i in range(TOGETHER):
        cols = slice(i * HD, (i + 1) * HD)
        pieces = stale_pieces(k_ref, v_ref, bias_ref, cols)
        pieces.append((kf_ref[:, cols], vf_ref[:, cols], bias_ref[KEYS:]))
        result, level = attend(q_ref[:, cols], pieces, 1, 1)
        h = g * TOGETHER + i
        out_ref[pl.ds(pl.multiple_of(h * CAP, 32), CAP), :] = result
        stat = add_stat(stat, level, h)

    def finish():
        out_ref[HEADS_HERE * CAP:, :] = stat_rows(stat_ref[...])

    collect(stat_ref, stat, finish)


STEPS = HEADS_HERE // TOGETHER


def column(rows, skip=0):
    return pl.BlockSpec((rows, TOGETHER * HD), lambda g: (0, g + skip))


def whole(*shape):
    return pl.BlockSpec(shape, lambda g: (0,) * len(shape))


def cost(rows, keys):
    return pl.CostEstimate(
        flops=4 * rows * keys * GROUP,
        bytes_accessed=4 * keys * GROUP,
        transcendentals=rows * keys * HEADS_HERE,
    )


def attend_others(place, q, kv, bias):
    rows = (NY - 1) * CAP
    return pl.pallas_call(
        others_kernel,
        grid=(STEPS,),
        in_specs=[
            pl.BlockSpec(memory_space=pltpu.SMEM),
            pl.BlockSpec((NY, CAP, TOGETHER * HD), lambda g: (0, 0, g)),
            column(KEYS), column(KEYS, STEPS), whole(KEYS + CAP, HD),
        ],
        out_specs=whole(NY, RETURNED, HD),
        out_shape=jax.ShapeDtypeStruct((NY, RETURNED, HD), bf16),
        scratch_shapes=[pltpu.VMEM((rows, HD), f32)],
        compiler_params=params(60),
        cost_estimate=cost(rows, KEYS),
    )(place, q, kv, kv, bias)


def attend_own(q, kv, kf, vf, bias):
    return pl.pallas_call(
        own_kernel,
        grid=(STEPS,),
        in_specs=[
            column(CAP), column(KEYS), column(KEYS, STEPS), column(CAP), column(CAP), whole(KEYS + CAP, HD),
        ],
        out_specs=whole(RETURNED, HD),
        out_shape=jax.ShapeDtypeStruct((RETURNED, HD), bf16),
        scratch_shapes=[pltpu.VMEM((CAP, HD), f32)],
        compiler_params=params(40),
        cost_estimate=cost(CAP, KEYS + CAP),
    )(q, kv, kv, kf, vf, bias)


def project_kernel(place_ref, part_ref, own_ref, w_ref, out_ref):
    def part(b, rows):
        return jnp.where(place_ref[1] == b, own_ref[rows, :].astype(f32), part_ref[b, rows, :].astype(f32))

    stats = [part(b, slice(HEADS_HERE * CAP, RETURNED)) for b in range(NY)]
    shares = []
    for h in range(HEADS_HERE):
        levels = [s[3 * h:3 * h + 1] + s[3 * h + 1:3 * h + 2] + s[3 * h + 2:3 * h + 3] for s in stats]
        top = levels[0]
        for level in levels[1:]:
            top = jnp.maximum(top, level)
        weights = [jnp.exp2(level - top) for level in levels]
        total = weights[0]
        for weight in weights[1:]:
            total = total + weight
        shares += [weight / total for weight in weights]
    shares = jnp.concatenate(shares + [jnp.zeros((HD - len(shares), HD), f32)], axis=0).T
    heads = []
    for h in range(HEADS_HERE):
        accum = jnp.zeros((CAP, HD), f32)
        for b in range(NY):
            share = shares[:CAP, h * NY + b:h * NY + b + 1]
            accum = accum + share * part(b, slice(h * CAP, (h + 1) * CAP))
        heads.append(accum.astype(bf16))
    attended = jnp.concatenate(heads, axis=1)
    half = D // 2
    step = 384
    mask = lower_half((8, step))
    for j in range(half // step):
        left = jnp.dot(attended, w_ref[:, j * step:(j + 1) * step], preferred_element_type=f32)
        right = jnp.dot(attended, w_ref[:, half + j * step:half + (j + 1) * step], preferred_element_type=f32)
        for s in range(NHEAD):
            k = s // 2
            a = left[64 + 8 * k:72 + 8 * k]
            b = right[64 + 8 * k:72 + 8 * k]
            if s % 2 == 0:
                rest = jnp.where(mask, a, pltpu.roll(b, 4, 0))
            else:
                rest = jnp.where(mask, pltpu.roll(a, 4, 0), b)
            pieces = (
                (j * step, left[8 * s:8 * s + 8]),
                (half + j * step, right[8 * s:8 * s + 8]),
                (D + j * step, rest),
            )
            for col, tile in pieces:
                row = 8 * (col // OUT_PACKED)
                col = col % OUT_PACKED
                assert col + step <= OUT_PACKED
                out_ref[s, row:row + 8, col:col + step] = tile.astype(bf16)


def project(place, parts, own, w):
    return pl.pallas_call(
        project_kernel,
        in_specs=[pl.BlockSpec(memory_space=pltpu.SMEM)] + [pl.BlockSpec(memory_space=pltpu.VMEM)] * 3,
        out_specs=pl.BlockSpec(memory_space=pltpu.VMEM),
        out_shape=jax.ShapeDtypeStruct((NHEAD, 16, OUT_PACKED), bf16),
        compiler_params=params(24),
    )(place, parts, own, w)


def mix_kernel(limit_ref, in_ref, hidden_ref, gate_ref, out_ref):
    total = in_ref[0].astype(f32)
    for s in range(1, NHEAD):
        total = total + in_ref[s].astype(f32)
    flat = jnp.concatenate([total[0:8], total[8:16]], axis=1)
    half = D // 2
    rest = flat[:, D:]
    tail = jnp.concatenate([rest[0:4], rest[4:8]], axis=1)
    projected = jnp.concatenate([flat[:, :D], tail], axis=0)
    residual = hidden_ref[...].astype(f32)
    live = lax.broadcasted_iota(jnp.int32, (OWN, D), 0) < limit_ref[0]
    mixed = jnp.where(live, residual + gate_ref[...] * projected, residual)
    out_ref[...] = mixed.astype(bf16)


def mix(limit, received, hidden, gate):
    vmem = pl.BlockSpec(memory_space=pltpu.VMEM)
    return pl.pallas_call(
        mix_kernel,
        in_specs=[pl.BlockSpec(memory_space=pltpu.SMEM), vmem, vmem, vmem],
        out_specs=vmem,
        out_shape=jax.ShapeDtypeStruct((OWN, D), bf16),
        compiler_params=params(16),
    )(limit, received, hidden, gate)


def swap(x, axis):
    return lax.all_to_all(x, axis, split_axis=0, concat_axis=0, tiled=True)


def local(fq, fk, fv, sk, sv, lengths, hidden, gate, w):
    z, yh, c = (lax.axis_index(a) for a in ("z", "yh", "c"))
    own_head = lax.axis_index("yl") * NX + lax.axis_index("x")

    place = jnp.stack([z, yh, c]).astype(jnp.int32)
    kv = lax.all_gather(jnp.concatenate([sk, sv], axis=1), ("z", "c"), axis=0, tiled=True)
    query, kf, vf, bias = unpack(place, lengths, swap(pack(fq, fk, fv), HEAD))
    queries = lax.all_gather(query, "yh", axis=0)
    returned = swap(attend_others(place, queries, kv, bias), "yh")
    own = attend_own(query, kv, kf, vf, bias)
    packed = project(place, returned, own, w)
    own_length = lax.dynamic_index_in_dim(lengths, (z * NY + yh) * NC + c, 0, keepdims=False)
    limit = jnp.clip(own_length - own_head * OWN, 0, OWN)[None]
    return mix(limit, swap(packed, HEAD), hidden, gate[None, :])


def solution(mesh):
    grid = Mesh(mesh.devices.reshape(NZ, NY, NC, NYL, NX), ALL)
    rows = P(ALL, None)
    stale = P(("z", "yh", "c"), HEAD)
    in_specs = (rows, rows, rows, stale, stale, P(), rows, P(), P(HEAD, None))
    return jax.shard_map(local, mesh=grid, in_specs=in_specs, out_specs=rows, check_vma=False)
```

```python
import jax
import jax.numpy as jnp
import numpy as np
from jax import lax
from jax.experimental import pallas as pl
from jax.experimental.pallas import tpu as pltpu
from jax.sharding import Mesh, PartitionSpec as P

HD = 128
CAP = 96
NZ, NY, NC, NYL, NX = 8, 4, 2, 2, 4
NHEAD = NYL * NX
GROUP = 512
HEADS_HERE = GROUP // HD
OWN = 12
D = 3072
KEYS = NZ * NC * CAP
QUERIES = NY * CAP
BIG = -1e30
TOGETHER = 2
STAT_ROWS = 16
RETURNED = HEADS_HERE * CAP + STAT_ROWS
EXP2_SCALE = float(np.log2(np.e) * HD ** (-0.5))
HEAD = ("yl", "x")
ALL = ("z", "yh", "c", "yl", "x")
f32 = jnp.float32
bf16 = jnp.bfloat16
PACKED = 3 * 768 // 2
OUT_PACKED = (D + D // 2) // 2


def params(mb):
    return pltpu.CompilerParams(vmem_limit_bytes=mb * 2**20)


def lower_half(shape):
    return lax.broadcasted_iota(jnp.int32, shape, 0) < 4


def pack_kernel(q_ref, k_ref, v_ref, out_ref):
    mask = lower_half((8, GROUP // 2))
    for h in range(NHEAD):
        tops, rests = [], []
        for ref in (q_ref, k_ref, v_ref):
            rows = ref[:, h * GROUP:(h + 1) * GROUP].astype(f32)
            tops.append(rows[0:8])
            tail = rows[4:12]
            first = pltpu.roll(tail[:, : GROUP // 2], 4, 0)
            rests.append(jnp.where(mask, first, tail[:, GROUP // 2:]))
        flat = jnp.concatenate(tops + rests, axis=1)
        both = jnp.concatenate([flat[:, :PACKED], flat[:, PACKED:]], axis=0)
        out_ref[h] = both.astype(bf16)


def pack(fq, fk, fv):
    return pl.pallas_call(
        pack_kernel,
        out_shape=jax.ShapeDtypeStruct((NHEAD, 16, PACKED), bf16),
        compiler_params=params(60),
    )(fq, fk, fv)


def unpack_kernel(lengths_ref, in_ref, q_ref, k_ref, v_ref, bias_ref):
    mask = lower_half((8, GROUP // 2))
    tops = [[], [], []]
    rests = [[], [], []]
    for s in range(NHEAD):
        both = in_ref[s].astype(f32)
        flat = jnp.concatenate([both[0:8], both[8:16]], axis=1)
        for i in range(3):
            tops[i].append(flat[:, i * GROUP:(i + 1) * GROUP])
            base = 3 * GROUP + i * (GROUP // 2)
            rests[i].append(flat[:, base:base + GROUP // 2])
    for i, ref in enumerate((q_ref, k_ref, v_ref)):
        tiles = list(tops[i])
        for k in range(NHEAD // 2):
            a, b = rests[i][2 * k], rests[i][2 * k + 1]
            left = jnp.where(mask, a, pltpu.roll(b, 4, 0))
            right = jnp.where(mask, pltpu.roll(a, 4, 0), b)
            tiles.append(jnp.concatenate([left, right], axis=1))
        ref[...] = jnp.concatenate(tiles, axis=0).astype(bf16)

    z, yh, c = (lax.axis_index(a) for a in ("z", "yh", "c"))
    row = lax.broadcasted_iota(jnp.int32, (CAP, HD), 0)
    mine = lax.broadcasted_iota(jnp.int32, (CAP, HD), 1) == 1
    for j in range(NZ * NC):
        length = lengths_ref[(j // NC) * NY * NC + yh * NC + j % NC]
        hidden_length = jnp.where((j // NC == z) & (j % NC == c), 0, length)
        seen = row < jnp.where(mine, hidden_length, length)
        bias_ref[j * CAP:(j + 1) * CAP] = jnp.where(seen, 0.0, BIG).astype(bf16)
    rest = row - 64
    token = jnp.where(row < 64, 12 * (row >> 3) + (row & 7), 12 * (rest >> 2) + 8 + (rest & 3))
    own_length = lengths_ref[z * NY * NC + yh * NC + c]
    seen = token < jnp.where(mine, own_length, 0)
    bias_ref[KEYS:] = jnp.where(seen, 0.0, BIG).astype(bf16)


def unpack(lengths, received):
    one = jax.ShapeDtypeStruct((CAP, GROUP), bf16)
    smem = pl.BlockSpec(memory_space=pltpu.SMEM)
    vmem = pl.BlockSpec(memory_space=pltpu.VMEM)
    return pl.pallas_call(
        unpack_kernel,
        in_specs=[smem, vmem],
        out_specs=(vmem,) * 4,
        out_shape=(one, one, one, jax.ShapeDtypeStruct((KEYS + CAP, HD), bf16)),
        compiler_params=params(16),
    )(lengths, received)


def attend(load_query, keys, hot_lane, count):
    rows = count * CAP
    hot = (lax.broadcasted_iota(jnp.int32, (rows, HD), 1) == hot_lane).astype(f32).astype(bf16)
    query = jnp.concatenate([load_query, hot], axis=1)
    scores = []
    for key, _, bias in keys:
        key = jnp.concatenate([key, bias], axis=1)
        scores.append(lax.dot_general(query, key, (((1,), (1,)), ((), ())), preferred_element_type=f32))
    top = scores[0].max(axis=1, keepdims=True)
    for s in scores[1:]:
        top = jnp.maximum(top, s.max(axis=1, keepdims=True))
    total = jnp.zeros((rows, 1), f32)
    accum = jnp.zeros((rows, HD), f32)
    for s, (_, value, _) in zip(scores, keys):
        weights = jnp.exp2((s - top) * EXP2_SCALE)
        total = total + weights.sum(axis=1, keepdims=True)
        accum = accum + jnp.dot(weights.astype(bf16), value, preferred_element_type=f32)
    return (accum / total).astype(bf16), top * EXP2_SCALE + jnp.log2(total)


def add_stat(stat, level, h):
    lane = lax.broadcasted_iota(jnp.int32, stat.shape, 1)
    hi = level.astype(bf16).astype(f32)
    mid = (level - hi).astype(bf16).astype(f32)
    low = level - hi - mid
    stat = jnp.where(lane == 3 * h, hi, stat)
    stat = jnp.where(lane == 3 * h + 1, mid, stat)
    return jnp.where(lane == 3 * h + 2, low, stat)


def stale_pieces(k_ref, v_ref, bias_ref, cols):
    chunk = KEYS // 4
    return [
        (k_ref[j:j + chunk, cols], v_ref[j:j + chunk, cols], bias_ref[j:j + chunk])
        for j in range(0, KEYS, chunk)
    ]


def stat_rows(stat):
    square = jnp.concatenate([stat, jnp.zeros((HD - CAP, HD), f32)], axis=0)
    return square.T[:STAT_ROWS].astype(bf16)


def collect(stat_ref, stat, finish):
    g = pl.program_id(0)

    @pl.when(g == 0)
    def _():
        stat_ref[...] = stat

    @pl.when(g != 0)
    def _():
        stat_ref[...] = stat_ref[...] + stat

    pl.when(g == pl.num_programs(0) - 1)(finish)


def others_kernel(q_ref, k_ref, v_ref, bias_ref, out_ref, stat_ref):
    g = pl.program_id(0)
    yh = lax.axis_index("yh")
    count = NY - 1
    slots = [lax.rem(yh + k, NY) for k in range(1, NY)]
    stat = jnp.zeros((count * CAP, HD), f32)

    @pl.when(g == 0)
    def _():
        out_ref[yh] = jnp.zeros((RETURNED, HD), bf16)

    for i in range(TOGETHER):
        cols = slice(i * HD, (i + 1) * HD)
        query = jnp.concatenate([q_ref[slot, :, cols] for slot in slots], axis=0)
        result, level = attend(query, stale_pieces(k_ref, v_ref, bias_ref, cols), 0, count)
        h = g * TOGETHER + i
        for n, slot in enumerate(slots):
            out_ref[slot, pl.ds(pl.multiple_of(h * CAP, 32), CAP), :] = result[n * CAP:(n + 1) * CAP]
        stat = add_stat(stat, level, h)

    def finish():
        for n, slot in enumerate(slots):
            out_ref[slot, HEADS_HERE * CAP:, :] = stat_rows(stat_ref[n * CAP:(n + 1) * CAP])

    collect(stat_ref, stat, finish)


def own_kernel(q_ref, k_ref, v_ref, kf_ref, vf_ref, bias_ref, out_ref, stat_ref):
    g = pl.program_id(0)
    stat = jnp.zeros((CAP, HD), f32)
    for i in range(TOGETHER):
        cols = slice(i * HD, (i + 1) * HD)
        pieces = stale_pieces(k_ref, v_ref, bias_ref, cols)
        pieces.append((kf_ref[:, cols], vf_ref[:, cols], bias_ref[KEYS:]))
        result, level = attend(q_ref[:, cols], pieces, 1, 1)
        h = g * TOGETHER + i
        out_ref[pl.ds(pl.multiple_of(h * CAP, 32), CAP), :] = result
        stat = add_stat(stat, level, h)

    def finish():
        out_ref[HEADS_HERE * CAP:, :] = stat_rows(stat_ref[...])

    collect(stat_ref, stat, finish)


STEPS = HEADS_HERE // TOGETHER


def column(rows, skip=0):
    return pl.BlockSpec((rows, TOGETHER * HD), lambda g: (0, g + skip))


def whole(*shape):
    return pl.BlockSpec(shape, lambda g: (0,) * len(shape))


def cost(rows, keys):
    return pl.CostEstimate(
        flops=4 * rows * keys * GROUP,
        bytes_accessed=4 * keys * GROUP,
        transcendentals=rows * keys * HEADS_HERE,
    )


def attend_others(q, kv, bias):
    rows = (NY - 1) * CAP
    return pl.pallas_call(
        others_kernel,
        grid=(STEPS,),
        in_specs=[
            pl.BlockSpec((NY, CAP, TOGETHER * HD), lambda g: (0, 0, g)),
            column(KEYS), column(KEYS, STEPS), whole(KEYS + CAP, HD),
        ],
        out_specs=whole(NY, RETURNED, HD),
        out_shape=jax.ShapeDtypeStruct((NY, RETURNED, HD), bf16),
        scratch_shapes=[pltpu.VMEM((rows, HD), f32)],
        compiler_params=params(60),
        cost_estimate=cost(rows, KEYS),
    )(q, kv, kv, bias)


def attend_own(q, kv, kf, vf, bias):
    return pl.pallas_call(
        own_kernel,
        grid=(STEPS,),
        in_specs=[
            column(CAP), column(KEYS), column(KEYS, STEPS), column(CAP), column(CAP), whole(KEYS + CAP, HD),
        ],
        out_specs=whole(RETURNED, HD),
        out_shape=jax.ShapeDtypeStruct((RETURNED, HD), bf16),
        scratch_shapes=[pltpu.VMEM((CAP, HD), f32)],
        compiler_params=params(60),
        cost_estimate=cost(CAP, KEYS + CAP),
    )(q, kv, kv, kf, vf, bias)


def project_kernel(part_ref, own_ref, w_hbm, out_ref, w_ref, sem):
    copy = pltpu.make_async_copy(w_hbm, w_ref, sem)
    copy.start()
    yh = lax.axis_index("yh")

    def part(b, rows):
        return jnp.where(yh == b, own_ref[rows, :].astype(f32), part_ref[b, rows, :].astype(f32))

    stats = [part(b, slice(HEADS_HERE * CAP, RETURNED)) for b in range(NY)]
    shares = []
    for h in range(HEADS_HERE):
        levels = [s[3 * h:3 * h + 1] + s[3 * h + 1:3 * h + 2] + s[3 * h + 2:3 * h + 3] for s in stats]
        top = levels[0]
        for level in levels[1:]:
            top = jnp.maximum(top, level)
        weights = [jnp.exp2(level - top) for level in levels]
        total = weights[0]
        for weight in weights[1:]:
            total = total + weight
        shares += [weight / total for weight in weights]
    shares = jnp.concatenate(shares + [jnp.zeros((HD - len(shares), HD), f32)], axis=0).T
    heads = []
    for h in range(HEADS_HERE):
        accum = jnp.zeros((CAP, HD), f32)
        for b in range(NY):
            share = shares[:CAP, h * NY + b:h * NY + b + 1]
            accum = accum + share * part(b, slice(h * CAP, (h + 1) * CAP))
        heads.append(accum.astype(bf16))
    attended = jnp.concatenate(heads, axis=1)
    copy.wait()
    half = D // 2
    step = 384
    mask = lower_half((8, step))
    for j in range(half // step):
        left = jnp.dot(attended, w_ref[:, j * step:(j + 1) * step], preferred_element_type=f32)
        right = jnp.dot(attended, w_ref[:, half + j * step:half + (j + 1) * step], preferred_element_type=f32)
        for s in range(NHEAD):
            k = s // 2
            a = left[64 + 8 * k:72 + 8 * k]
            b = right[64 + 8 * k:72 + 8 * k]
            if s % 2 == 0:
                rest = jnp.where(mask, a, pltpu.roll(b, 4, 0))
            else:
                rest = jnp.where(mask, pltpu.roll(a, 4, 0), b)
            pieces = (
                (j * step, left[8 * s:8 * s + 8]),
                (half + j * step, right[8 * s:8 * s + 8]),
                (D + j * step, rest),
            )
            for col, tile in pieces:
                row = 8 * (col // OUT_PACKED)
                col = col % OUT_PACKED
                assert col + step <= OUT_PACKED
                out_ref[s, row:row + 8, col:col + step] = tile.astype(bf16)


def project(parts, own, w):
    return pl.pallas_call(
        project_kernel,
        in_specs=[pl.BlockSpec(memory_space=pltpu.VMEM)] * 2 + [pl.BlockSpec(memory_space=pl.ANY)],
        out_specs=pl.BlockSpec(memory_space=pltpu.VMEM),
        out_shape=jax.ShapeDtypeStruct((NHEAD, 16, OUT_PACKED), bf16),
        scratch_shapes=[pltpu.VMEM((GROUP, D), bf16), pltpu.SemaphoreType.DMA],
        compiler_params=params(60),
    )(parts, own, w)


def mix_kernel(lengths_ref, in_ref, hidden_ref, gate_ref, out_ref):
    total = in_ref[0].astype(f32)
    for s in range(1, NHEAD):
        total = total + in_ref[s].astype(f32)
    flat = jnp.concatenate([total[0:8], total[8:16]], axis=1)
    half = D // 2
    rest = flat[:, D:]
    tail = jnp.concatenate([rest[0:4], rest[4:8]], axis=1)
    projected = jnp.concatenate([flat[:, :D], tail], axis=0)
    residual = hidden_ref[...].astype(f32)
    patch = (lax.axis_index("z") * NY + lax.axis_index("yh")) * NC + lax.axis_index("c")
    limit = lengths_ref[patch] - (lax.axis_index("yl") * NX + lax.axis_index("x")) * OWN
    live = lax.broadcasted_iota(jnp.int32, (OWN, D), 0) < limit
    mixed = jnp.where(live, residual + gate_ref[...] * projected, residual)
    out_ref[...] = mixed.astype(bf16)


def mix(lengths, received, hidden, gate):
    vmem = pl.BlockSpec(memory_space=pltpu.VMEM)
    return pl.pallas_call(
        mix_kernel,
        in_specs=[pl.BlockSpec(memory_space=pltpu.SMEM), vmem, vmem, vmem],
        out_specs=vmem,
        out_shape=jax.ShapeDtypeStruct((OWN, D), bf16),
        compiler_params=params(16),
    )(lengths, received, hidden, gate)


def swap(x, axis):
    return lax.all_to_all(x, axis, split_axis=0, concat_axis=0, tiled=True)


def local(fq, fk, fv, sk, sv, lengths, hidden, gate, w):
    kv = lax.all_gather(jnp.concatenate([sk, sv], axis=1), ("z", "c"), axis=0, tiled=True)
    query, kf, vf, bias = unpack(lengths, swap(pack(fq, fk, fv), HEAD))
    queries = lax.all_gather(query, "yh", axis=0)
    returned = swap(attend_others(queries, kv, bias), "yh")
    own = attend_own(query, kv, kf, vf, bias)
    packed = project(returned, own, w)
    return mix(lengths, swap(packed, HEAD), hidden, gate[None, :])


def solution(mesh):
    grid = Mesh(mesh.devices.reshape(NZ, NY, NC, NYL, NX), ALL)
    rows = P(ALL, None)
    stale = P(("z", "yh", "c"), HEAD)
    in_specs = (rows, rows, rows, stale, stale, P(), rows, P(), P(HEAD, None))
    return jax.shard_map(local, mesh=grid, in_specs=in_specs, out_specs=rows, check_vma=False)
```

```python
import jax
import jax.numpy as jnp
import numpy as np
from jax import lax
from jax.experimental import pallas as pl
from jax.experimental.pallas import tpu as pltpu
from jax.sharding import Mesh, PartitionSpec as P

HD = 128
CAP = 96
NZ, NY, NC, NYL, NX = 8, 4, 2, 2, 4
NHEAD = NYL * NX
GROUP = 512
HEADS_HERE = GROUP // HD
OWN = 12
D = 3072
KEYS = NZ * NC * CAP
QUERIES = NY * CAP
BIG = -1e30
TOGETHER = 2
STAT_ROWS = 16
RETURNED = HEADS_HERE * CAP + STAT_ROWS
EXP2_SCALE = float(np.log2(np.e) * HD ** (-0.5))
HEAD = ("yl", "x")
ALL = ("z", "yh", "c", "yl", "x")
f32 = jnp.float32
bf16 = jnp.bfloat16
PACKED = 3 * 768 // 2
OUT_PACKED = (D + D // 2) // 2


def params(mb):
    return pltpu.CompilerParams(vmem_limit_bytes=mb * 2**20)


def lower_half(shape):
    return lax.broadcasted_iota(jnp.int32, shape, 0) < 4


def pack_kernel(q_ref, k_ref, v_ref, out_ref):
    mask = lower_half((8, GROUP // 2))
    for h in range(NHEAD):
        tops, rests = [], []
        for ref in (q_ref, k_ref, v_ref):
            rows = ref[:, h * GROUP:(h + 1) * GROUP].astype(f32)
            tops.append(rows[0:8])
            tail = rows[4:12]
            first = pltpu.roll(tail[:, : GROUP // 2], 4, 0)
            rests.append(jnp.where(mask, first, tail[:, GROUP // 2:]))
        flat = jnp.concatenate(tops + rests, axis=1)
        both = jnp.concatenate([flat[:, :PACKED], flat[:, PACKED:]], axis=0)
        out_ref[h] = both.astype(bf16)


def pack(fq, fk, fv):
    return pl.pallas_call(
        pack_kernel,
        out_shape=jax.ShapeDtypeStruct((NHEAD, 16, PACKED), bf16),
        compiler_params=params(60),
    )(fq, fk, fv)


def unpack_kernel(lengths_ref, in_ref, q_ref, k_ref, v_ref, bias_ref, live_ref):
    mask = lower_half((8, GROUP // 2))
    tops = [[], [], []]
    rests = [[], [], []]
    for s in range(NHEAD):
        both = in_ref[s].astype(f32)
        flat = jnp.concatenate([both[0:8], both[8:16]], axis=1)
        for i in range(3):
            tops[i].append(flat[:, i * GROUP:(i + 1) * GROUP])
            base = 3 * GROUP + i * (GROUP // 2)
            rests[i].append(flat[:, base:base + GROUP // 2])
    for i, ref in enumerate((q_ref, k_ref, v_ref)):
        tiles = list(tops[i])
        for k in range(NHEAD // 2):
            a, b = rests[i][2 * k], rests[i][2 * k + 1]
            left = jnp.where(mask, a, pltpu.roll(b, 4, 0))
            right = jnp.where(mask, pltpu.roll(a, 4, 0), b)
            tiles.append(jnp.concatenate([left, right], axis=1))
        ref[...] = jnp.concatenate(tiles, axis=0).astype(bf16)

    z, yh, c = (lax.axis_index(a) for a in ("z", "yh", "c"))
    row = lax.broadcasted_iota(jnp.int32, (CAP, HD), 0)
    mine = lax.broadcasted_iota(jnp.int32, (CAP, HD), 1) == 1
    for j in range(NZ * NC):
        length = lengths_ref[(j // NC) * NY * NC + yh * NC + j % NC]
        hidden_length = jnp.where((j // NC == z) & (j % NC == c), 0, length)
        seen = row < jnp.where(mine, hidden_length, length)
        bias_ref[j * CAP:(j + 1) * CAP] = jnp.where(seen, 0.0, BIG).astype(bf16)
    rest = row - 64
    token = jnp.where(row < 64, 12 * (row >> 3) + (row & 7), 12 * (rest >> 2) + 8 + (rest & 3))
    own_length = lengths_ref[z * NY * NC + yh * NC + c]
    seen = token < jnp.where(mine, own_length, 0)
    bias_ref[KEYS:] = jnp.where(seen, 0.0, BIG).astype(bf16)
    first = (lax.axis_index("yl") * NX + lax.axis_index("x")) * OWN
    slot = first + lax.broadcasted_iota(jnp.int32, (16, HD), 0)
    live_ref[...] = jnp.where(slot < own_length, 1.0, 0.0)


def unpack(lengths, received):
    one = jax.ShapeDtypeStruct((CAP, GROUP), bf16)
    smem = pl.BlockSpec(memory_space=pltpu.SMEM)
    vmem = pl.BlockSpec(memory_space=pltpu.VMEM)
    return pl.pallas_call(
        unpack_kernel,
        in_specs=[smem, vmem],
        out_specs=(vmem,) * 5,
        out_shape=(
            one, one, one,
            jax.ShapeDtypeStruct((KEYS + CAP, HD), bf16), jax.ShapeDtypeStruct((16, HD), f32),
        ),
        compiler_params=params(16),
    )(lengths, received)


def attend(load_query, keys, hot_lane, count):
    rows = count * CAP
    hot = (lax.broadcasted_iota(jnp.int32, (rows, HD), 1) == hot_lane).astype(f32).astype(bf16)
    query = jnp.concatenate([load_query, hot], axis=1)
    scores = []
    for key, _, bias in keys:
        key = jnp.concatenate([key, bias], axis=1)
        scores.append(lax.dot_general(query, key, (((1,), (1,)), ((), ())), preferred_element_type=f32))
    top = scores[0].max(axis=1, keepdims=True)
    for s in scores[1:]:
        top = jnp.maximum(top, s.max(axis=1, keepdims=True))
    total = jnp.zeros((rows, 1), f32)
    accum = jnp.zeros((rows, HD), f32)
    for s, (_, value, _) in zip(scores, keys):
        weights = jnp.exp2((s - top) * EXP2_SCALE)
        total = total + weights.sum(axis=1, keepdims=True)
        accum = accum + jnp.dot(weights.astype(bf16), value, preferred_element_type=f32)
    return (accum / total).astype(bf16), top * EXP2_SCALE + jnp.log2(total)


def add_stat(stat, level, h):
    lane = lax.broadcasted_iota(jnp.int32, stat.shape, 1)
    hi = level.astype(bf16).astype(f32)
    mid = (level - hi).astype(bf16).astype(f32)
    low = level - hi - mid
    stat = jnp.where(lane == 3 * h, hi, stat)
    stat = jnp.where(lane == 3 * h + 1, mid, stat)
    return jnp.where(lane == 3 * h + 2, low, stat)


def stale_pieces(k_ref, v_ref, bias_ref, cols):
    chunk = KEYS // 4
    return [
        (k_ref[j:j + chunk, cols], v_ref[j:j + chunk, cols], bias_ref[j:j + chunk])
        for j in range(0, KEYS, chunk)
    ]


def stat_rows(stat):
    square = jnp.concatenate([stat, jnp.zeros((HD - CAP, HD), f32)], axis=0)
    return square.T[:STAT_ROWS].astype(bf16)


def collect(stat_ref, stat, finish):
    g = pl.program_id(0)

    @pl.when(g == 0)
    def _():
        stat_ref[...] = stat

    @pl.when(g != 0)
    def _():
        stat_ref[...] = stat_ref[...] + stat

    pl.when(g == pl.num_programs(0) - 1)(finish)


def others_kernel(q_ref, k_ref, v_ref, bias_ref, out_ref, stat_ref):
    g = pl.program_id(0)
    yh = lax.axis_index("yh")
    count = NY - 1
    slots = [lax.rem(yh + k, NY) for k in range(1, NY)]
    stat = jnp.zeros((count * CAP, HD), f32)

    @pl.when(g == 0)
    def _():
        out_ref[yh] = jnp.zeros((RETURNED, HD), bf16)

    for i in range(TOGETHER):
        cols = slice(i * HD, (i + 1) * HD)
        query = jnp.concatenate([q_ref[slot, :, cols] for slot in slots], axis=0)
        result, level = attend(query, stale_pieces(k_ref, v_ref, bias_ref, cols), 0, count)
        h = g * TOGETHER + i
        for n, slot in enumerate(slots):
            out_ref[slot, pl.ds(pl.multiple_of(h * CAP, 32), CAP), :] = result[n * CAP:(n + 1) * CAP]
        stat = add_stat(stat, level, h)

    def finish():
        for n, slot in enumerate(slots):
            out_ref[slot, HEADS_HERE * CAP:, :] = stat_rows(stat_ref[n * CAP:(n + 1) * CAP])

    collect(stat_ref, stat, finish)


def own_kernel(q_ref, k_ref, v_ref, kf_ref, vf_ref, bias_ref, w_ref, out_ref, staged_ref, stat_ref, sem):
    g = pl.program_id(0)
    copy = pltpu.make_async_copy(w_ref, staged_ref, sem)

    @pl.when(g == 0)
    def _():
        copy.start()

    stat = jnp.zeros((CAP, HD), f32)
    for i in range(TOGETHER):
        cols = slice(i * HD, (i + 1) * HD)
        pieces = stale_pieces(k_ref, v_ref, bias_ref, cols)
        pieces.append((kf_ref[:, cols], vf_ref[:, cols], bias_ref[KEYS:]))
        result, level = attend(q_ref[:, cols], pieces, 1, 1)
        h = g * TOGETHER + i
        out_ref[pl.ds(pl.multiple_of(h * CAP, 32), CAP), :] = result
        stat = add_stat(stat, level, h)

    def finish():
        out_ref[HEADS_HERE * CAP:, :] = stat_rows(stat_ref[...])
        copy.wait()

    collect(stat_ref, stat, finish)


STEPS = HEADS_HERE // TOGETHER


def column(rows, skip=0):
    return pl.BlockSpec((rows, TOGETHER * HD), lambda g: (0, g + skip))


def whole(*shape):
    return pl.BlockSpec(shape, lambda g: (0,) * len(shape))


def cost(rows, keys):
    return pl.CostEstimate(
        flops=4 * rows * keys * GROUP,
        bytes_accessed=4 * keys * GROUP,
        transcendentals=rows * keys * HEADS_HERE,
    )


def attend_others(q, kv, bias):
    rows = (NY - 1) * CAP
    return pl.pallas_call(
        others_kernel,
        grid=(STEPS,),
        in_specs=[
            pl.BlockSpec((NY, CAP, TOGETHER * HD), lambda g: (0, 0, g)),
            column(KEYS), column(KEYS, STEPS), whole(KEYS + CAP, HD),
        ],
        out_specs=whole(NY, RETURNED, HD),
        out_shape=jax.ShapeDtypeStruct((NY, RETURNED, HD), bf16),
        scratch_shapes=[pltpu.VMEM((rows, HD), f32)],
        compiler_params=params(60),
        cost_estimate=cost(rows, KEYS),
    )(q, kv, kv, bias)


def attend_own(q, kv, kf, vf, bias, w):
    return pl.pallas_call(
        own_kernel,
        grid=(STEPS,),
        in_specs=[
            column(CAP), column(KEYS), column(KEYS, STEPS), column(CAP), column(CAP), whole(KEYS + CAP, HD),
            pl.BlockSpec(memory_space=pltpu.HBM),
        ],
        out_specs=(whole(RETURNED, HD), pl.BlockSpec(memory_space=pl.ANY)),
        out_shape=(pltpu.VMEM((RETURNED, HD), bf16), pltpu.VMEM((GROUP, D), bf16)),
        scratch_shapes=[pltpu.VMEM((CAP, HD), f32), pltpu.SemaphoreType.DMA],
        compiler_params=params(56),
        cost_estimate=cost(CAP, KEYS + CAP),
    )(q, kv, kv, kf, vf, bias, w)


def project_kernel(part_ref, own_ref, w_ref, out_ref):
    yh = lax.axis_index("yh")

    def part(b, rows):
        return jnp.where(yh == b, own_ref[rows, :].astype(f32), part_ref[b, rows, :].astype(f32))

    stats = [part(b, slice(HEADS_HERE * CAP, RETURNED)) for b in range(NY)]
    shares = []
    for h in range(HEADS_HERE):
        levels = [s[3 * h:3 * h + 1] + s[3 * h + 1:3 * h + 2] + s[3 * h + 2:3 * h + 3] for s in stats]
        top = levels[0]
        for level in levels[1:]:
            top = jnp.maximum(top, level)
        weights = [jnp.exp2(level - top) for level in levels]
        total = weights[0]
        for weight in weights[1:]:
            total = total + weight
        shares += [weight / total for weight in weights]
    shares = jnp.concatenate(shares + [jnp.zeros((HD - len(shares), HD), f32)], axis=0).T
    heads = []
    for h in range(HEADS_HERE):
        accum = jnp.zeros((CAP, HD), f32)
        for b in range(NY):
            share = shares[:CAP, h * NY + b:h * NY + b + 1]
            accum = accum + share * part(b, slice(h * CAP, (h + 1) * CAP))
        heads.append(accum.astype(bf16))
    attended = jnp.concatenate(heads, axis=1)
    half = D // 2
    step = 384
    mask = lower_half((8, step))
    for j in range(half // step):
        left = jnp.dot(attended, w_ref[:, j * step:(j + 1) * step], preferred_element_type=f32)
        right = jnp.dot(attended, w_ref[:, half + j * step:half + (j + 1) * step], preferred_element_type=f32)
        for s in range(NHEAD):
            k = s // 2
            a = left[64 + 8 * k:72 + 8 * k]
            b = right[64 + 8 * k:72 + 8 * k]
            if s % 2 == 0:
                rest = jnp.where(mask, a, pltpu.roll(b, 4, 0))
            else:
                rest = jnp.where(mask, pltpu.roll(a, 4, 0), b)
            pieces = (
                (j * step, left[8 * s:8 * s + 8]),
                (half + j * step, right[8 * s:8 * s + 8]),
                (D + j * step, rest),
            )
            for col, tile in pieces:
                row = 8 * (col // OUT_PACKED)
                col = col % OUT_PACKED
                assert col + step <= OUT_PACKED
                out_ref[s, row:row + 8, col:col + step] = tile.astype(bf16)


def project(parts, own, w):
    return pl.pallas_call(
        project_kernel,
        in_specs=[pl.BlockSpec(memory_space=pltpu.VMEM)] * 3,
        out_specs=pl.BlockSpec(memory_space=pltpu.VMEM),
        out_shape=jax.ShapeDtypeStruct((NHEAD, 16, OUT_PACKED), bf16),
        compiler_params=params(24),
    )(parts, own, w)


def mix_kernel(live_ref, in_ref, hidden_ref, gate_ref, out_ref):
    total = in_ref[0].astype(f32)
    for s in range(1, NHEAD):
        total = total + in_ref[s].astype(f32)
    flat = jnp.concatenate([total[0:8], total[8:16]], axis=1)
    half = D // 2
    rest = flat[:, D:]
    tail = jnp.concatenate([rest[0:4], rest[4:8]], axis=1)
    projected = jnp.concatenate([flat[:, :D], tail], axis=0)
    residual = hidden_ref[...].astype(f32)
    live = live_ref[:OWN, :1] > 0.5
    mixed = jnp.where(live, residual + gate_ref[...] * projected, residual)
    out_ref[...] = mixed.astype(bf16)


def mix(live, received, hidden, gate):
    vmem = pl.BlockSpec(memory_space=pltpu.VMEM)
    return pl.pallas_call(
        mix_kernel,
        in_specs=[vmem] * 4,
        out_specs=vmem,
        out_shape=jax.ShapeDtypeStruct((OWN, D), bf16),
        compiler_params=params(16),
    )(live, received, hidden, gate)


def swap(x, axis):
    return lax.all_to_all(x, axis, split_axis=0, concat_axis=0, tiled=True)


def local(fq, fk, fv, sk, sv, lengths, hidden, gate, w):
    kv = lax.all_gather(jnp.concatenate([sk, sv], axis=1), ("z", "c"), axis=0, tiled=True)
    query, kf, vf, bias, live = unpack(lengths, swap(pack(fq, fk, fv), HEAD))
    queries = lax.all_gather(query, "yh", axis=0)
    returned = swap(attend_others(queries, kv, bias), "yh")
    own, staged = attend_own(query, kv, kf, vf, bias, w)
    packed = project(returned, own, staged)
    return mix(live, swap(packed, HEAD), hidden, gate[None, :])


def solution(mesh):
    grid = Mesh(mesh.devices.reshape(NZ, NY, NC, NYL, NX), ALL)
    rows = P(ALL, None)
    stale = P(("z", "yh", "c"), HEAD)
    in_specs = (rows, rows, rows, stale, stale, P(), rows, P(), P(HEAD, None))
    return jax.shard_map(local, mesh=grid, in_specs=in_specs, out_specs=rows, check_vma=False)
```

```python
import jax
import jax.numpy as jnp
import numpy as np
from jax import lax
from jax.experimental import pallas as pl
from jax.experimental.pallas import tpu as pltpu
from jax.sharding import Mesh, PartitionSpec as P

HD = 128
CAP = 96
NZ, NY, NC, NYL, NX = 8, 4, 2, 2, 4
NHEAD = NYL * NX
GROUP = 512
HEADS_HERE = GROUP // HD
OWN = 12
D = 3072
KEYS = NZ * NC * CAP
QUERIES = NY * CAP
BIG = -1e30
TOGETHER = 2
STAT_ROWS = 16
RETURNED = HEADS_HERE * CAP + STAT_ROWS
EXP2_SCALE = float(np.log2(np.e) * HD ** (-0.5))
HEAD = ("yl", "x")
ALL = ("z", "yh", "c", "yl", "x")
f32 = jnp.float32
bf16 = jnp.bfloat16
PACKED = 3 * 768 // 2
OUT_PACKED = (D + D // 2) // 2


def params(mb):
    return pltpu.CompilerParams(vmem_limit_bytes=mb * 2**20)


def lower_half(shape):
    return lax.broadcasted_iota(jnp.int32, shape, 0) < 4


def pack_kernel(q_ref, k_ref, v_ref, out_ref):
    mask = lower_half((8, GROUP // 2))
    for h in range(NHEAD):
        tops, rests = [], []
        for ref in (q_ref, k_ref, v_ref):
            rows = ref[:, h * GROUP:(h + 1) * GROUP].astype(f32)
            tops.append(rows[0:8])
            tail = rows[4:12]
            first = pltpu.roll(tail[:, : GROUP // 2], 4, 0)
            rests.append(jnp.where(mask, first, tail[:, GROUP // 2:]))
        flat = jnp.concatenate(tops + rests, axis=1)
        both = jnp.concatenate([flat[:, :PACKED], flat[:, PACKED:]], axis=0)
        out_ref[h] = both.astype(bf16)


def pack(fq, fk, fv):
    return pl.pallas_call(
        pack_kernel,
        out_shape=jax.ShapeDtypeStruct((NHEAD, 16, PACKED), bf16),
        compiler_params=params(60),
    )(fq, fk, fv)


def unpack_kernel(lengths_ref, in_ref, q_ref, k_ref, v_ref, bias_ref, live_ref):
    mask = lower_half((8, GROUP // 2))
    tops = [[], [], []]
    rests = [[], [], []]
    for s in range(NHEAD):
        both = in_ref[s].astype(f32)
        flat = jnp.concatenate([both[0:8], both[8:16]], axis=1)
        for i in range(3):
            tops[i].append(flat[:, i * GROUP:(i + 1) * GROUP])
            base = 3 * GROUP + i * (GROUP // 2)
            rests[i].append(flat[:, base:base + GROUP // 2])
    for i, ref in enumerate((q_ref, k_ref, v_ref)):
        tiles = list(tops[i])
        for k in range(NHEAD // 2):
            a, b = rests[i][2 * k], rests[i][2 * k + 1]
            left = jnp.where(mask, a, pltpu.roll(b, 4, 0))
            right = jnp.where(mask, pltpu.roll(a, 4, 0), b)
            tiles.append(jnp.concatenate([left, right], axis=1))
        ref[...] = jnp.concatenate(tiles, axis=0).astype(bf16)

    z, yh, c = (lax.axis_index(a) for a in ("z", "yh", "c"))
    row = lax.broadcasted_iota(jnp.int32, (CAP, HD), 0)
    mine = lax.broadcasted_iota(jnp.int32, (CAP, HD), 1) == 1
    for j in range(NZ * NC):
        length = lengths_ref[(j // NC) * NY * NC + yh * NC + j % NC]
        hidden_length = jnp.where((j // NC == z) & (j % NC == c), 0, length)
        seen = row < jnp.where(mine, hidden_length, length)
        bias_ref[j * CAP:(j + 1) * CAP] = jnp.where(seen, 0.0, BIG).astype(bf16)
    rest = row - 64
    token = jnp.where(row < 64, 12 * (row >> 3) + (row & 7), 12 * (rest >> 2) + 8 + (rest & 3))
    own_length = lengths_ref[z * NY * NC + yh * NC + c]
    seen = token < jnp.where(mine, own_length, 0)
    bias_ref[KEYS:] = jnp.where(seen, 0.0, BIG).astype(bf16)
    first = (lax.axis_index("yl") * NX + lax.axis_index("x")) * OWN
    slot = first + lax.broadcasted_iota(jnp.int32, (16, HD), 0)
    live_ref[...] = jnp.where(slot < own_length, 1.0, 0.0)


def unpack(lengths, received):
    one = jax.ShapeDtypeStruct((CAP, GROUP), bf16)
    smem = pl.BlockSpec(memory_space=pltpu.SMEM)
    vmem = pl.BlockSpec(memory_space=pltpu.VMEM)
    return pl.pallas_call(
        unpack_kernel,
        in_specs=[smem, vmem],
        out_specs=(vmem,) * 5,
        out_shape=(
            one, one, one,
            jax.ShapeDtypeStruct((KEYS + CAP, HD), bf16), jax.ShapeDtypeStruct((16, HD), f32),
        ),
        compiler_params=params(16),
    )(lengths, received)


def attend(load_query, keys, hot_lane, count):
    rows = count * CAP
    hot = (lax.broadcasted_iota(jnp.int32, (rows, HD), 1) == hot_lane).astype(f32).astype(bf16)
    query = jnp.concatenate([load_query, hot], axis=1)
    scores = []
    for key, _, bias in keys:
        key = jnp.concatenate([key, bias], axis=1)
        scores.append(lax.dot_general(query, key, (((1,), (1,)), ((), ())), preferred_element_type=f32))
    top = scores[0].max(axis=1, keepdims=True)
    for s in scores[1:]:
        top = jnp.maximum(top, s.max(axis=1, keepdims=True))
    total = jnp.zeros((rows, 1), f32)
    accum = jnp.zeros((rows, HD), f32)
    for s, (_, value, _) in zip(scores, keys):
        weights = jnp.exp2((s - top) * EXP2_SCALE)
        total = total + weights.sum(axis=1, keepdims=True)
        accum = accum + jnp.dot(weights.astype(bf16), value, preferred_element_type=f32)
    return (accum / total).astype(bf16), top * EXP2_SCALE + jnp.log2(total)


def add_stat(stat, level, h):
    lane = lax.broadcasted_iota(jnp.int32, stat.shape, 1)
    hi = level.astype(bf16).astype(f32)
    mid = (level - hi).astype(bf16).astype(f32)
    low = level - hi - mid
    stat = jnp.where(lane == 3 * h, hi, stat)
    stat = jnp.where(lane == 3 * h + 1, mid, stat)
    return jnp.where(lane == 3 * h + 2, low, stat)


def stale_pieces(k_ref, v_ref, bias_ref, cols, parts=4):
    chunk = KEYS // parts
    return [
        (k_ref[j:j + chunk, cols], v_ref[j:j + chunk, cols], bias_ref[j:j + chunk])
        for j in range(0, KEYS, chunk)
    ]


def stat_rows(stat):
    square = jnp.concatenate([stat, jnp.zeros((HD - CAP, HD), f32)], axis=0)
    return square.T[:STAT_ROWS].astype(bf16)


def collect(stat_ref, stat, finish):
    g = pl.program_id(0)

    @pl.when(g == 0)
    def _():
        stat_ref[...] = stat

    @pl.when(g != 0)
    def _():
        stat_ref[...] = stat_ref[...] + stat

    pl.when(g == pl.num_programs(0) - 1)(finish)


def others_kernel(q_hbm, kv_hbm, bias_hbm, out_ref, q_ref, k_ref, v_ref, bias_ref, sems):
    copies = [
        pltpu.make_async_copy(kv_hbm.at[:, :GROUP], k_ref, sems.at[0]),
        pltpu.make_async_copy(kv_hbm.at[:, GROUP:], v_ref, sems.at[1]),
        pltpu.make_async_copy(q_hbm, q_ref, sems.at[2]),
        pltpu.make_async_copy(bias_hbm, bias_ref, sems.at[3]),
    ]
    for copy in copies:
        copy.start()
    yh = lax.axis_index("yh")
    count = NY - 1
    slots = [lax.rem(yh + k, NY) for k in range(1, NY)]
    stat = jnp.zeros((count * CAP, HD), f32)
    out_ref[yh] = jnp.zeros((RETURNED, HD), bf16)
    for copy in copies:
        copy.wait()
    for h in range(HEADS_HERE):
        cols = slice(h * HD, (h + 1) * HD)
        query = jnp.concatenate([q_ref[slot, :, cols] for slot in slots], axis=0)
        result, level = attend(query, stale_pieces(k_ref, v_ref, bias_ref, cols, 3), 0, count)
        for n, slot in enumerate(slots):
            out_ref[slot, h * CAP:(h + 1) * CAP, :] = result[n * CAP:(n + 1) * CAP]
        stat = add_stat(stat, level, h)
    for n, slot in enumerate(slots):
        out_ref[slot, HEADS_HERE * CAP:, :] = stat_rows(stat[n * CAP:(n + 1) * CAP])


def own_kernel(q_ref, k_ref, v_ref, kf_ref, vf_ref, bias_ref, w_ref, out_ref, staged_ref, stat_ref, sem):
    g = pl.program_id(0)
    copy = pltpu.make_async_copy(w_ref, staged_ref, sem)

    @pl.when(g == 0)
    def _():
        copy.start()

    stat = jnp.zeros((CAP, HD), f32)
    for i in range(TOGETHER):
        cols = slice(i * HD, (i + 1) * HD)
        pieces = stale_pieces(k_ref, v_ref, bias_ref, cols)
        pieces.append((kf_ref[:, cols], vf_ref[:, cols], bias_ref[KEYS:]))
        result, level = attend(q_ref[:, cols], pieces, 1, 1)
        h = g * TOGETHER + i
        out_ref[pl.ds(pl.multiple_of(h * CAP, 32), CAP), :] = result
        stat = add_stat(stat, level, h)

    def finish():
        out_ref[HEADS_HERE * CAP:, :] = stat_rows(stat_ref[...])
        copy.wait()

    collect(stat_ref, stat, finish)


STEPS = HEADS_HERE // TOGETHER


def column(rows, skip=0):
    return pl.BlockSpec((rows, TOGETHER * HD), lambda g: (0, g + skip))


def whole(*shape):
    return pl.BlockSpec(shape, lambda g: (0,) * len(shape))


def cost(rows, keys):
    return pl.CostEstimate(
        flops=4 * rows * keys * GROUP,
        bytes_accessed=4 * keys * GROUP,
        transcendentals=rows * keys * HEADS_HERE,
    )


def attend_others(q, kv, bias):
    return pl.pallas_call(
        others_kernel,
        in_specs=[pl.BlockSpec(memory_space=pl.ANY), pl.BlockSpec(memory_space=pltpu.HBM), pl.BlockSpec(memory_space=pl.ANY)],
        out_specs=pl.BlockSpec(memory_space=pltpu.VMEM),
        out_shape=jax.ShapeDtypeStruct((NY, RETURNED, HD), bf16),
        scratch_shapes=[
            pltpu.VMEM((NY, CAP, GROUP), bf16),
            pltpu.VMEM((KEYS, GROUP), bf16), pltpu.VMEM((KEYS, GROUP), bf16),
            pltpu.VMEM((KEYS + CAP, HD), bf16),
            pltpu.SemaphoreType.DMA((4,)),
        ],
        compiler_params=params(60),
        cost_estimate=cost((NY - 1) * CAP, KEYS),
    )(q, kv, bias)


def attend_own(q, kv, kf, vf, bias, w):
    return pl.pallas_call(
        own_kernel,
        grid=(STEPS,),
        in_specs=[
            column(CAP), column(KEYS), column(KEYS, STEPS), column(CAP), column(CAP), whole(KEYS + CAP, HD),
            pl.BlockSpec(memory_space=pltpu.HBM),
        ],
        out_specs=(whole(RETURNED, HD), pl.BlockSpec(memory_space=pl.ANY)),
        out_shape=(pltpu.VMEM((RETURNED, HD), bf16), pltpu.VMEM((GROUP, D), bf16)),
        scratch_shapes=[pltpu.VMEM((CAP, HD), f32), pltpu.SemaphoreType.DMA],
        compiler_params=params(44),
        cost_estimate=cost(CAP, KEYS + CAP),
    )(q, kv, kv, kf, vf, bias, w)


def project_kernel(part_ref, own_ref, w_ref, out_ref):
    yh = lax.axis_index("yh")

    def part(b, rows):
        return jnp.where(yh == b, own_ref[rows, :].astype(f32), part_ref[b, rows, :].astype(f32))

    stats = [part(b, slice(HEADS_HERE * CAP, RETURNED)) for b in range(NY)]
    shares = []
    for h in range(HEADS_HERE):
        levels = [s[3 * h:3 * h + 1] + s[3 * h + 1:3 * h + 2] + s[3 * h + 2:3 * h + 3] for s in stats]
        top = levels[0]
        for level in levels[1:]:
            top = jnp.maximum(top, level)
        weights = [jnp.exp2(level - top) for level in levels]
        total = weights[0]
        for weight in weights[1:]:
            total = total + weight
        shares += [weight / total for weight in weights]
    shares = jnp.concatenate(shares + [jnp.zeros((HD - len(shares), HD), f32)], axis=0).T
    heads = []
    for h in range(HEADS_HERE):
        accum = jnp.zeros((CAP, HD), f32)
        for b in range(NY):
            share = shares[:CAP, h * NY + b:h * NY + b + 1]
            accum = accum + share * part(b, slice(h * CAP, (h + 1) * CAP))
        heads.append(accum.astype(bf16))
    attended = jnp.concatenate(heads, axis=1)
    half = D // 2
    step = 384
    mask = lower_half((8, step))
    for j in range(half // step):
        left = jnp.dot(attended, w_ref[:, j * step:(j + 1) * step], preferred_element_type=f32)
        right = jnp.dot(attended, w_ref[:, half + j * step:half + (j + 1) * step], preferred_element_type=f32)
        for s in range(NHEAD):
            k = s // 2
            a = left[64 + 8 * k:72 + 8 * k]
            b = right[64 + 8 * k:72 + 8 * k]
            if s % 2 == 0:
                rest = jnp.where(mask, a, pltpu.roll(b, 4, 0))
            else:
                rest = jnp.where(mask, pltpu.roll(a, 4, 0), b)
            pieces = (
                (j * step, left[8 * s:8 * s + 8]),
                (half + j * step, right[8 * s:8 * s + 8]),
                (D + j * step, rest),
            )
            for col, tile in pieces:
                row = 8 * (col // OUT_PACKED)
                col = col % OUT_PACKED
                assert col + step <= OUT_PACKED
                out_ref[s, row:row + 8, col:col + step] = tile.astype(bf16)


def project(parts, own, w):
    return pl.pallas_call(
        project_kernel,
        in_specs=[pl.BlockSpec(memory_space=pltpu.VMEM)] * 3,
        out_specs=pl.BlockSpec(memory_space=pltpu.VMEM),
        out_shape=jax.ShapeDtypeStruct((NHEAD, 16, OUT_PACKED), bf16),
        compiler_params=params(24),
    )(parts, own, w)


def mix_kernel(live_ref, in_ref, hidden_ref, gate_ref, out_ref):
    total = in_ref[0].astype(f32)
    for s in range(1, NHEAD):
        total = total + in_ref[s].astype(f32)
    flat = jnp.concatenate([total[0:8], total[8:16]], axis=1)
    half = D // 2
    rest = flat[:, D:]
    tail = jnp.concatenate([rest[0:4], rest[4:8]], axis=1)
    projected = jnp.concatenate([flat[:, :D], tail], axis=0)
    residual = hidden_ref[...].astype(f32)
    live = live_ref[:OWN, :1] > 0.5
    mixed = jnp.where(live, residual + gate_ref[...] * projected, residual)
    out_ref[...] = mixed.astype(bf16)


def mix(live, received, hidden, gate):
    vmem = pl.BlockSpec(memory_space=pltpu.VMEM)
    return pl.pallas_call(
        mix_kernel,
        in_specs=[vmem] * 4,
        out_specs=vmem,
        out_shape=jax.ShapeDtypeStruct((OWN, D), bf16),
        compiler_params=params(16),
    )(live, received, hidden, gate)


def swap(x, axis):
    return lax.all_to_all(x, axis, split_axis=0, concat_axis=0, tiled=True)


def local(fq, fk, fv, sk, sv, lengths, hidden, gate, w):
    kv = lax.all_gather(jnp.concatenate([sk, sv], axis=1), ("z", "c"), axis=0, tiled=True)
    query, kf, vf, bias, live = unpack(lengths, swap(pack(fq, fk, fv), HEAD))
    queries = lax.all_gather(query, "yh", axis=0)
    returned = swap(attend_others(queries, kv, bias), "yh")
    own, staged = attend_own(query, kv, kf, vf, bias, w)
    packed = project(returned, own, staged)
    return mix(live, swap(packed, HEAD), hidden, gate[None, :])


def solution(mesh):
    grid = Mesh(mesh.devices.reshape(NZ, NY, NC, NYL, NX), ALL)
    rows = P(ALL, None)
    stale = P(("z", "yh", "c"), HEAD)
    in_specs = (rows, rows, rows, stale, stale, P(), rows, P(), P(HEAD, None))
    return jax.shard_map(local, mesh=grid, in_specs=in_specs, out_specs=rows, check_vma=False)
```

```python
import jax
import jax.numpy as jnp
import numpy as np
from jax import lax
from jax.experimental import pallas as pl
from jax.experimental.pallas import tpu as pltpu
from jax.sharding import Mesh, PartitionSpec as P

HD = 128
CAP = 96
NZ, NY, NC, NYL, NX = 8, 4, 2, 2, 4
NHEAD = NYL * NX
GROUP = 512
HEADS_HERE = GROUP // HD
OWN = 12
D = 3072
KEYS = NZ * NC * CAP
QUERIES = NY * CAP
BIG = -1e30
TOGETHER = 2
STAT_ROWS = 16
RETURNED = HEADS_HERE * CAP + STAT_ROWS
EXP2_SCALE = float(np.log2(np.e) * HD ** (-0.5))
HEAD = ("yl", "x")
ALL = ("z", "yh", "c", "yl", "x")
f32 = jnp.float32
bf16 = jnp.bfloat16
PACKED = 3 * 768 // 2
OUT_PACKED = (D + D // 2) // 2


def params(mb):
    return pltpu.CompilerParams(vmem_limit_bytes=mb * 2**20)


def lower_half(shape):
    return lax.broadcasted_iota(jnp.int32, shape, 0) < 4


def pack_kernel(q_ref, k_ref, v_ref, out_ref):
    mask = lower_half((8, GROUP // 2))
    for h in range(NHEAD):
        tops, rests = [], []
        for ref in (q_ref, k_ref, v_ref):
            rows = ref[:, h * GROUP:(h + 1) * GROUP].astype(f32)
            tops.append(rows[0:8])
            tail = rows[4:12]
            first = pltpu.roll(tail[:, : GROUP // 2], 4, 0)
            rests.append(jnp.where(mask, first, tail[:, GROUP // 2:]))
        flat = jnp.concatenate(tops + rests, axis=1)
        both = jnp.concatenate([flat[:, :PACKED], flat[:, PACKED:]], axis=0)
        out_ref[h] = both.astype(bf16)


def pack(fq, fk, fv):
    return pl.pallas_call(
        pack_kernel,
        out_shape=jax.ShapeDtypeStruct((NHEAD, 16, PACKED), bf16),
        compiler_params=params(60),
    )(fq, fk, fv)


def unpack_kernel(lengths_ref, in_ref, q_ref, k_ref, v_ref, bias_ref, live_ref):
    mask = lower_half((8, GROUP // 2))
    tops = [[], [], []]
    rests = [[], [], []]
    for s in range(NHEAD):
        both = in_ref[s].astype(f32)
        flat = jnp.concatenate([both[0:8], both[8:16]], axis=1)
        for i in range(3):
            tops[i].append(flat[:, i * GROUP:(i + 1) * GROUP])
            base = 3 * GROUP + i * (GROUP // 2)
            rests[i].append(flat[:, base:base + GROUP // 2])
    for i, ref in enumerate((q_ref, k_ref, v_ref)):
        tiles = list(tops[i])
        for k in range(NHEAD // 2):
            a, b = rests[i][2 * k], rests[i][2 * k + 1]
            left = jnp.where(mask, a, pltpu.roll(b, 4, 0))
            right = jnp.where(mask, pltpu.roll(a, 4, 0), b)
            tiles.append(jnp.concatenate([left, right], axis=1))
        ref[...] = jnp.concatenate(tiles, axis=0).astype(bf16)

    z, yh, c = (lax.axis_index(a) for a in ("z", "yh", "c"))
    row = lax.broadcasted_iota(jnp.int32, (CAP, HD), 0)
    mine = lax.broadcasted_iota(jnp.int32, (CAP, HD), 1) == 1
    for j in range(NZ * NC):
        length = lengths_ref[(j // NC) * NY * NC + yh * NC + j % NC]
        hidden_length = jnp.where((j // NC == z) & (j % NC == c), 0, length)
        seen = row < jnp.where(mine, hidden_length, length)
        bias_ref[j * CAP:(j + 1) * CAP] = jnp.where(seen, 0.0, BIG).astype(bf16)
    rest = row - 64
    token = jnp.where(row < 64, 12 * (row >> 3) + (row & 7), 12 * (rest >> 2) + 8 + (rest & 3))
    own_length = lengths_ref[z * NY * NC + yh * NC + c]
    seen = token < jnp.where(mine, own_length, 0)
    bias_ref[KEYS:] = jnp.where(seen, 0.0, BIG).astype(bf16)
    first = (lax.axis_index("yl") * NX + lax.axis_index("x")) * OWN
    slot = first + lax.broadcasted_iota(jnp.int32, (16, HD), 0)
    live_ref[...] = jnp.where(slot < own_length, 1.0, 0.0)


def unpack(lengths, received):
    one = jax.ShapeDtypeStruct((CAP, GROUP), bf16)
    smem = pl.BlockSpec(memory_space=pltpu.SMEM)
    vmem = pl.BlockSpec(memory_space=pltpu.VMEM)
    return pl.pallas_call(
        unpack_kernel,
        in_specs=[smem, vmem],
        out_specs=(vmem,) * 5,
        out_shape=(
            one, one, one,
            jax.ShapeDtypeStruct((KEYS + CAP, HD), bf16), jax.ShapeDtypeStruct((16, HD), f32),
        ),
        compiler_params=params(16),
    )(lengths, received)


def attend(load_query, keys, hot_lane, count):
    rows = count * CAP
    hot = (lax.broadcasted_iota(jnp.int32, (rows, HD), 1) == hot_lane).astype(f32).astype(bf16)
    query = jnp.concatenate([load_query, hot], axis=1)
    scores = []
    for key, _, bias in keys:
        key = jnp.concatenate([key, bias], axis=1)
        scores.append(lax.dot_general(query, key, (((1,), (1,)), ((), ())), preferred_element_type=f32))
    top = scores[0].max(axis=1, keepdims=True)
    for s in scores[1:]:
        top = jnp.maximum(top, s.max(axis=1, keepdims=True))
    total = jnp.zeros((rows, 1), f32)
    accum = jnp.zeros((rows, HD), f32)
    for s, (_, value, _) in zip(scores, keys):
        weights = jnp.exp2((s - top) * EXP2_SCALE)
        total = total + weights.sum(axis=1, keepdims=True)
        accum = accum + jnp.dot(weights.astype(bf16), value, preferred_element_type=f32)
    return (accum / total).astype(bf16), top * EXP2_SCALE + jnp.log2(total)


def add_stat(stat, level, h):
    lane = lax.broadcasted_iota(jnp.int32, stat.shape, 1)
    hi = level.astype(bf16).astype(f32)
    mid = (level - hi).astype(bf16).astype(f32)
    low = level - hi - mid
    stat = jnp.where(lane == 3 * h, hi, stat)
    stat = jnp.where(lane == 3 * h + 1, mid, stat)
    return jnp.where(lane == 3 * h + 2, low, stat)


def stale_pieces(k_ref, v_ref, bias_ref, cols, parts=4):
    chunk = KEYS // parts
    return [
        (k_ref[j:j + chunk, cols], v_ref[j:j + chunk, cols], bias_ref[j:j + chunk])
        for j in range(0, KEYS, chunk)
    ]


def stat_rows(stat):
    square = jnp.concatenate([stat, jnp.zeros((HD - CAP, HD), f32)], axis=0)
    return square.T[:STAT_ROWS].astype(bf16)


def collect(stat_ref, stat, finish):
    g = pl.program_id(0)

    @pl.when(g == 0)
    def _():
        stat_ref[...] = stat

    @pl.when(g != 0)
    def _():
        stat_ref[...] = stat_ref[...] + stat

    pl.when(g == pl.num_programs(0) - 1)(finish)


def others_kernel(q_hbm, kv_hbm, bias_hbm, out_ref, q_ref, k_ref, v_ref, bias_ref, sems):
    copies = [
        pltpu.make_async_copy(kv_hbm.at[:, :GROUP], k_ref, sems.at[0]),
        pltpu.make_async_copy(kv_hbm.at[:, GROUP:], v_ref, sems.at[1]),
        pltpu.make_async_copy(q_hbm, q_ref, sems.at[2]),
        pltpu.make_async_copy(bias_hbm, bias_ref, sems.at[3]),
    ]
    for copy in copies:
        copy.start()
    yh = lax.axis_index("yh")
    count = NY - 1
    slots = [lax.rem(yh + k, NY) for k in range(1, NY)]
    stat = jnp.zeros((count * CAP, HD), f32)
    out_ref[yh] = jnp.zeros((RETURNED, HD), bf16)
    for copy in copies:
        copy.wait()
    for h in range(HEADS_HERE):
        cols = slice(h * HD, (h + 1) * HD)
        query = jnp.concatenate([q_ref[slot, :, cols] for slot in slots], axis=0)
        result, level = attend(query, stale_pieces(k_ref, v_ref, bias_ref, cols, 3), 0, count)
        for n, slot in enumerate(slots):
            out_ref[slot, h * CAP:(h + 1) * CAP, :] = result[n * CAP:(n + 1) * CAP]
        stat = add_stat(stat, level, h)
    for n, slot in enumerate(slots):
        out_ref[slot, HEADS_HERE * CAP:, :] = stat_rows(stat[n * CAP:(n + 1) * CAP])


def own_kernel(q_ref, k_ref, v_ref, kf_ref, vf_ref, bias_ref, w_ref, out_ref, staged_ref, stat_ref, sem):
    g = pl.program_id(0)
    copy = pltpu.make_async_copy(w_ref, staged_ref, sem)

    @pl.when(g == 0)
    def _():
        copy.start()

    stat = jnp.zeros((CAP, HD), f32)
    for i in range(TOGETHER):
        cols = slice(i * HD, (i + 1) * HD)
        pieces = stale_pieces(k_ref, v_ref, bias_ref, cols)
        pieces.append((kf_ref[:, cols], vf_ref[:, cols], bias_ref[KEYS:]))
        result, level = attend(q_ref[:, cols], pieces, 1, 1)
        h = g * TOGETHER + i
        out_ref[pl.ds(pl.multiple_of(h * CAP, 32), CAP), :] = result
        stat = add_stat(stat, level, h)

    def finish():
        out_ref[HEADS_HERE * CAP:, :] = stat_rows(stat_ref[...])
        copy.wait()

    collect(stat_ref, stat, finish)


STEPS = HEADS_HERE // TOGETHER


def column(rows, skip=0):
    return pl.BlockSpec((rows, TOGETHER * HD), lambda g: (0, g + skip))


def whole(*shape):
    return pl.BlockSpec(shape, lambda g: (0,) * len(shape))


def cost(rows, keys):
    return pl.CostEstimate(
        flops=4 * rows * keys * GROUP,
        bytes_accessed=4 * keys * GROUP,
        transcendentals=rows * keys * HEADS_HERE,
    )


def attend_others(q, kv, bias):
    return pl.pallas_call(
        others_kernel,
        in_specs=[pl.BlockSpec(memory_space=pl.ANY), pl.BlockSpec(memory_space=pltpu.HBM), pl.BlockSpec(memory_space=pl.ANY)],
        out_specs=pl.BlockSpec(memory_space=pltpu.VMEM),
        out_shape=jax.ShapeDtypeStruct((NY, RETURNED, HD), bf16),
        scratch_shapes=[
            pltpu.VMEM((NY, CAP, GROUP), bf16),
            pltpu.VMEM((KEYS, GROUP), bf16), pltpu.VMEM((KEYS, GROUP), bf16),
            pltpu.VMEM((KEYS + CAP, HD), bf16),
            pltpu.SemaphoreType.DMA((4,)),
        ],
        compiler_params=params(60),
        cost_estimate=cost((NY - 1) * CAP, KEYS),
    )(q, kv, bias)


def attend_own(q, kv, kf, vf, bias, w):
    return pl.pallas_call(
        own_kernel,
        grid=(STEPS,),
        in_specs=[
            column(CAP), column(KEYS), column(KEYS, STEPS), column(CAP), column(CAP), whole(KEYS + CAP, HD),
            pl.BlockSpec(memory_space=pltpu.HBM),
        ],
        out_specs=(whole(RETURNED, HD), pl.BlockSpec(memory_space=pl.ANY)),
        out_shape=(pltpu.VMEM((RETURNED, HD), bf16), pltpu.VMEM((GROUP, D), bf16)),
        scratch_shapes=[pltpu.VMEM((CAP, HD), f32), pltpu.SemaphoreType.DMA],
        compiler_params=params(56),
        cost_estimate=cost(CAP, KEYS + CAP),
    )(q, kv, kv, kf, vf, bias, w)


def project_kernel(part_hbm, own_ref, w_ref, out_ref, part_ref, sem):
    copy = pltpu.make_async_copy(part_hbm, part_ref, sem)
    copy.start()
    yh = lax.axis_index("yh")

    def part(b, rows):
        return jnp.where(yh == b, own_ref[rows, :].astype(f32), part_ref[b, rows, :].astype(f32))

    copy.wait()
    stats = [part(b, slice(HEADS_HERE * CAP, RETURNED)) for b in range(NY)]
    shares = []
    for h in range(HEADS_HERE):
        levels = [s[3 * h:3 * h + 1] + s[3 * h + 1:3 * h + 2] + s[3 * h + 2:3 * h + 3] for s in stats]
        top = levels[0]
        for level in levels[1:]:
            top = jnp.maximum(top, level)
        weights = [jnp.exp2(level - top) for level in levels]
        total = weights[0]
        for weight in weights[1:]:
            total = total + weight
        shares += [weight / total for weight in weights]
    shares = jnp.concatenate(shares + [jnp.zeros((HD - len(shares), HD), f32)], axis=0).T
    heads = []
    for h in range(HEADS_HERE):
        accum = jnp.zeros((CAP, HD), f32)
        for b in range(NY):
            share = shares[:CAP, h * NY + b:h * NY + b + 1]
            accum = accum + share * part(b, slice(h * CAP, (h + 1) * CAP))
        heads.append(accum.astype(bf16))
    attended = jnp.concatenate(heads, axis=1)
    half = D // 2
    step = 384
    mask = lower_half((8, step))
    for j in range(half // step):
        left = jnp.dot(attended, w_ref[:, j * step:(j + 1) * step], preferred_element_type=f32)
        right = jnp.dot(attended, w_ref[:, half + j * step:half + (j + 1) * step], preferred_element_type=f32)
        for s in range(NHEAD):
            k = s // 2
            a = left[64 + 8 * k:72 + 8 * k]
            b = right[64 + 8 * k:72 + 8 * k]
            if s % 2 == 0:
                rest = jnp.where(mask, a, pltpu.roll(b, 4, 0))
            else:
                rest = jnp.where(mask, pltpu.roll(a, 4, 0), b)
            pieces = (
                (j * step, left[8 * s:8 * s + 8]),
                (half + j * step, right[8 * s:8 * s + 8]),
                (D + j * step, rest),
            )
            for col, tile in pieces:
                row = 8 * (col // OUT_PACKED)
                col = col % OUT_PACKED
                assert col + step <= OUT_PACKED
                out_ref[s, row:row + 8, col:col + step] = tile.astype(bf16)


def project(parts, own, w):
    return pl.pallas_call(
        project_kernel,
        in_specs=[pl.BlockSpec(memory_space=pltpu.HBM)] + [pl.BlockSpec(memory_space=pltpu.VMEM)] * 2,
        out_specs=pl.BlockSpec(memory_space=pltpu.VMEM),
        out_shape=jax.ShapeDtypeStruct((NHEAD, 16, OUT_PACKED), bf16),
        scratch_shapes=[pltpu.VMEM((NY, RETURNED, HD), bf16), pltpu.SemaphoreType.DMA],
        compiler_params=params(24),
    )(parts, own, w)


def mix_kernel(live_ref, in_ref, hidden_ref, gate_ref, out_ref):
    total = in_ref[0].astype(f32)
    for s in range(1, NHEAD):
        total = total + in_ref[s].astype(f32)
    flat = jnp.concatenate([total[0:8], total[8:16]], axis=1)
    half = D // 2
    rest = flat[:, D:]
    tail = jnp.concatenate([rest[0:4], rest[4:8]], axis=1)
    projected = jnp.concatenate([flat[:, :D], tail], axis=0)
    residual = hidden_ref[...].astype(f32)
    live = live_ref[:OWN, :1] > 0.5
    mixed = jnp.where(live, residual + gate_ref[...] * projected, residual)
    out_ref[...] = mixed.astype(bf16)


def mix(live, received, hidden, gate):
    vmem = pl.BlockSpec(memory_space=pltpu.VMEM)
    return pl.pallas_call(
        mix_kernel,
        in_specs=[vmem] * 4,
        out_specs=vmem,
        out_shape=jax.ShapeDtypeStruct((OWN, D), bf16),
        compiler_params=params(16),
    )(live, received, hidden, gate)


def swap(x, axis):
    return lax.all_to_all(x, axis, split_axis=0, concat_axis=0, tiled=True)


def local(fq, fk, fv, sk, sv, lengths, hidden, gate, w):
    kv = lax.all_gather(jnp.concatenate([sk, sv], axis=1), ("z", "c"), axis=0, tiled=True)
    query, kf, vf, bias, live = unpack(lengths, swap(pack(fq, fk, fv), HEAD))
    queries = lax.all_gather(query, "yh", axis=0)
    returned = swap(attend_others(queries, kv, bias), "yh")
    own, staged = attend_own(query, kv, kf, vf, bias, w)
    packed = project(returned, own, staged)
    return mix(live, swap(packed, HEAD), hidden, gate[None, :])


def solution(mesh):
    grid = Mesh(mesh.devices.reshape(NZ, NY, NC, NYL, NX), ALL)
    rows = P(ALL, None)
    stale = P(("z", "yh", "c"), HEAD)
    in_specs = (rows, rows, rows, stale, stale, P(), rows, P(), P(HEAD, None))
    return jax.shard_map(local, mesh=grid, in_specs=in_specs, out_specs=rows, check_vma=False)
```

```python
import jax
import jax.numpy as jnp
import numpy as np
from jax import lax
from jax.experimental import pallas as pl
from jax.experimental.pallas import tpu as pltpu
from jax.sharding import Mesh, PartitionSpec as P

HD = 128
CAP = 96
NZ, NY, NC, NYL, NX = 8, 4, 2, 2, 4
NHEAD = NYL * NX
GROUP = 512
HEADS_HERE = GROUP // HD
OWN = 12
D = 3072
KEYS = NZ * NC * CAP
QUERIES = NY * CAP
BIG = -1e30
TOGETHER = 2
STAT_ROWS = 16
RETURNED = HEADS_HERE * CAP + STAT_ROWS
EXP2_SCALE = float(np.log2(np.e) * HD ** (-0.5))
HEAD = ("yl", "x")
ALL = ("z", "yh", "c", "yl", "x")
f32 = jnp.float32
bf16 = jnp.bfloat16
PACKED = 3 * 768 // 2
OUT_PACKED = (D + D // 2) // 2


def params(mb):
    return pltpu.CompilerParams(vmem_limit_bytes=mb * 2**20)


def lower_half(shape):
    return lax.broadcasted_iota(jnp.int32, shape, 0) < 4


def pack_kernel(q_ref, k_ref, v_ref, out_ref):
    mask = lower_half((8, GROUP // 2))
    for h in range(NHEAD):
        tops, rests = [], []
        for ref in (q_ref, k_ref, v_ref):
            rows = ref[:, h * GROUP:(h + 1) * GROUP].astype(f32)
            tops.append(rows[0:8])
            tail = rows[4:12]
            first = pltpu.roll(tail[:, : GROUP // 2], 4, 0)
            rests.append(jnp.where(mask, first, tail[:, GROUP // 2:]))
        flat = jnp.concatenate(tops + rests, axis=1)
        both = jnp.concatenate([flat[:, :PACKED], flat[:, PACKED:]], axis=0)
        out_ref[h] = both.astype(bf16)


def pack(fq, fk, fv):
    return pl.pallas_call(
        pack_kernel,
        out_shape=jax.ShapeDtypeStruct((NHEAD, 16, PACKED), bf16),
        compiler_params=params(60),
    )(fq, fk, fv)


def unpack_kernel(lengths_ref, in_ref, q_ref, k_ref, v_ref, bias_ref, live_ref):
    mask = lower_half((8, GROUP // 2))
    tops = [[], [], []]
    rests = [[], [], []]
    for s in range(NHEAD):
        both = in_ref[s].astype(f32)
        flat = jnp.concatenate([both[0:8], both[8:16]], axis=1)
        for i in range(3):
            tops[i].append(flat[:, i * GROUP:(i + 1) * GROUP])
            base = 3 * GROUP + i * (GROUP // 2)
            rests[i].append(flat[:, base:base + GROUP // 2])
    for i, ref in enumerate((q_ref, k_ref, v_ref)):
        tiles = list(tops[i])
        for k in range(NHEAD // 2):
            a, b = rests[i][2 * k], rests[i][2 * k + 1]
            left = jnp.where(mask, a, pltpu.roll(b, 4, 0))
            right = jnp.where(mask, pltpu.roll(a, 4, 0), b)
            tiles.append(jnp.concatenate([left, right], axis=1))
        ref[...] = jnp.concatenate(tiles, axis=0).astype(bf16)

    z, yh, c = (lax.axis_index(a) for a in ("z", "yh", "c"))
    row = lax.broadcasted_iota(jnp.int32, (CAP, HD), 0)
    mine = lax.broadcasted_iota(jnp.int32, (CAP, HD), 1) == 1
    for j in range(NZ * NC):
        length = lengths_ref[(j // NC) * NY * NC + yh * NC + j % NC]
        hidden_length = jnp.where((j // NC == z) & (j % NC == c), 0, length)
        seen = row < jnp.where(mine, hidden_length, length)
        bias_ref[j * CAP:(j + 1) * CAP] = jnp.where(seen, 0.0, BIG).astype(bf16)
    rest = row - 64
    token = jnp.where(row < 64, 12 * (row >> 3) + (row & 7), 12 * (rest >> 2) + 8 + (rest & 3))
    own_length = lengths_ref[z * NY * NC + yh * NC + c]
    seen = token < jnp.where(mine, own_length, 0)
    bias_ref[KEYS:] = jnp.where(seen, 0.0, BIG).astype(bf16)
    first = (lax.axis_index("yl") * NX + lax.axis_index("x")) * OWN
    slot = first + lax.broadcasted_iota(jnp.int32, (16, HD), 0)
    live_ref[...] = jnp.where(slot < own_length, 1.0, 0.0)


def unpack(lengths, received):
    one = jax.ShapeDtypeStruct((CAP, GROUP), bf16)
    smem = pl.BlockSpec(memory_space=pltpu.SMEM)
    vmem = pl.BlockSpec(memory_space=pltpu.VMEM)
    return pl.pallas_call(
        unpack_kernel,
        in_specs=[smem, vmem],
        out_specs=(vmem,) * 5,
        out_shape=(
            one, one, one,
            jax.ShapeDtypeStruct((KEYS + CAP, HD), bf16), jax.ShapeDtypeStruct((16, HD), f32),
        ),
        compiler_params=params(16),
    )(lengths, received)


def attend(load_query, keys, hot_lane, count):
    rows = count * CAP
    hot = (lax.broadcasted_iota(jnp.int32, (rows, HD), 1) == hot_lane).astype(f32).astype(bf16)
    query = jnp.concatenate([load_query, hot], axis=1)
    scores = []
    for key, _, bias in keys:
        key = jnp.concatenate([key, bias], axis=1)
        scores.append(lax.dot_general(query, key, (((1,), (1,)), ((), ())), preferred_element_type=f32))
    top = scores[0].max(axis=1, keepdims=True)
    for s in scores[1:]:
        top = jnp.maximum(top, s.max(axis=1, keepdims=True))
    total = jnp.zeros((rows, 1), f32)
    accum = jnp.zeros((rows, HD), f32)
    for s, (_, value, _) in zip(scores, keys):
        weights = jnp.exp2((s - top) * EXP2_SCALE)
        total = total + weights.sum(axis=1, keepdims=True)
        accum = accum + jnp.dot(weights.astype(bf16), value, preferred_element_type=f32)
    return (accum / total).astype(bf16), top * EXP2_SCALE + jnp.log2(total)


def add_stat(stat, level, h):
    lane = lax.broadcasted_iota(jnp.int32, stat.shape, 1)
    hi = level.astype(bf16).astype(f32)
    mid = (level - hi).astype(bf16).astype(f32)
    low = level - hi - mid
    stat = jnp.where(lane == 3 * h, hi, stat)
    stat = jnp.where(lane == 3 * h + 1, mid, stat)
    return jnp.where(lane == 3 * h + 2, low, stat)


def stale_pieces(k_ref, v_ref, bias_ref, cols, parts=4):
    chunk = KEYS // parts
    return [
        (k_ref[j:j + chunk, cols], v_ref[j:j + chunk, cols], bias_ref[j:j + chunk])
        for j in range(0, KEYS, chunk)
    ]


def stat_rows(stat):
    square = jnp.concatenate([stat, jnp.zeros((HD - CAP, HD), f32)], axis=0)
    return square.T[:STAT_ROWS].astype(bf16)


def collect(stat_ref, stat, finish):
    g = pl.program_id(0)

    @pl.when(g == 0)
    def _():
        stat_ref[...] = stat

    @pl.when(g != 0)
    def _():
        stat_ref[...] = stat_ref[...] + stat

    pl.when(g == pl.num_programs(0) - 1)(finish)


def others_kernel(q_hbm, kv_hbm, bias_hbm, out_ref, q_ref, k_ref, v_ref, bias_ref, sems):
    copies = [
        pltpu.make_async_copy(kv_hbm.at[:, :GROUP], k_ref, sems.at[0]),
        pltpu.make_async_copy(kv_hbm.at[:, GROUP:], v_ref, sems.at[1]),
        pltpu.make_async_copy(q_hbm, q_ref, sems.at[2]),
        pltpu.make_async_copy(bias_hbm, bias_ref, sems.at[3]),
    ]
    for copy in copies:
        copy.start()
    yh = lax.axis_index("yh")
    count = NY - 1
    slots = [lax.rem(yh + k, NY) for k in range(1, NY)]
    stat = jnp.zeros((count * CAP, HD), f32)
    out_ref[yh] = jnp.zeros((RETURNED, HD), bf16)
    for copy in copies:
        copy.wait()
    for h in range(HEADS_HERE):
        cols = slice(h * HD, (h + 1) * HD)
        query = jnp.concatenate([q_ref[slot, :, cols] for slot in slots], axis=0)
        result, level = attend(query, stale_pieces(k_ref, v_ref, bias_ref, cols, 3), 0, count)
        for n, slot in enumerate(slots):
            out_ref[slot, h * CAP:(h + 1) * CAP, :] = result[n * CAP:(n + 1) * CAP]
        stat = add_stat(stat, level, h)
    for n, slot in enumerate(slots):
        out_ref[slot, HEADS_HERE * CAP:, :] = stat_rows(stat[n * CAP:(n + 1) * CAP])


def own_kernel(q_ref, k_ref, v_ref, kf_ref, vf_ref, bias_ref, w_ref, out_ref, staged_ref, stat_ref, sem):
    g = pl.program_id(0)
    copy = pltpu.make_async_copy(w_ref, staged_ref, sem)

    @pl.when(g == 0)
    def _():
        copy.start()

    stat = jnp.zeros((CAP, HD), f32)
    for i in range(TOGETHER):
        cols = slice(i * HD, (i + 1) * HD)
        pieces = stale_pieces(k_ref, v_ref, bias_ref, cols)
        pieces.append((kf_ref[:, cols], vf_ref[:, cols], bias_ref[KEYS:]))
        result, level = attend(q_ref[:, cols], pieces, 1, 1)
        h = g * TOGETHER + i
        out_ref[pl.ds(pl.multiple_of(h * CAP, 32), CAP), :] = result
        stat = add_stat(stat, level, h)

    def finish():
        out_ref[HEADS_HERE * CAP:, :] = stat_rows(stat_ref[...])
        copy.wait()

    collect(stat_ref, stat, finish)


STEPS = HEADS_HERE // TOGETHER


def column(rows, skip=0):
    return pl.BlockSpec((rows, TOGETHER * HD), lambda g: (0, g + skip))


def whole(*shape):
    return pl.BlockSpec(shape, lambda g: (0,) * len(shape))


def cost(rows, keys):
    return pl.CostEstimate(
        flops=4 * rows * keys * GROUP,
        bytes_accessed=4 * keys * GROUP,
        transcendentals=rows * keys * HEADS_HERE,
    )


def attend_others(q, kv, bias):
    return pl.pallas_call(
        others_kernel,
        in_specs=[pl.BlockSpec(memory_space=pl.ANY), pl.BlockSpec(memory_space=pltpu.HBM), pl.BlockSpec(memory_space=pl.ANY)],
        out_specs=pl.BlockSpec(memory_space=pltpu.VMEM),
        out_shape=jax.ShapeDtypeStruct((NY, RETURNED, HD), bf16),
        scratch_shapes=[
            pltpu.VMEM((NY, CAP, GROUP), bf16),
            pltpu.VMEM((KEYS, GROUP), bf16), pltpu.VMEM((KEYS, GROUP), bf16),
            pltpu.VMEM((KEYS + CAP, HD), bf16),
            pltpu.SemaphoreType.DMA((4,)),
        ],
        compiler_params=params(60),
        cost_estimate=cost((NY - 1) * CAP, KEYS),
    )(q, kv, bias)


def attend_own(q, kv, kf, vf, bias, w):
    return pl.pallas_call(
        own_kernel,
        grid=(STEPS,),
        in_specs=[
            column(CAP), column(KEYS), column(KEYS, STEPS), column(CAP), column(CAP), whole(KEYS + CAP, HD),
            pl.BlockSpec(memory_space=pltpu.HBM),
        ],
        out_specs=(whole(RETURNED, HD), pl.BlockSpec(memory_space=pl.ANY)),
        out_shape=(pltpu.HBM((RETURNED, HD), bf16), pltpu.VMEM((GROUP, D), bf16)),
        scratch_shapes=[pltpu.VMEM((CAP, HD), f32), pltpu.SemaphoreType.DMA],
        compiler_params=params(56),
        cost_estimate=cost(CAP, KEYS + CAP),
    )(q, kv, kv, kf, vf, bias, w)


def project_kernel(part_hbm, own_hbm, w_ref, out_ref, part_ref, own_ref, sems):
    copies = [
        pltpu.make_async_copy(part_hbm, part_ref, sems.at[0]),
        pltpu.make_async_copy(own_hbm, own_ref, sems.at[1]),
    ]
    for copy in copies:
        copy.start()
    yh = lax.axis_index("yh")

    def part(b, rows):
        return jnp.where(yh == b, own_ref[rows, :].astype(f32), part_ref[b, rows, :].astype(f32))

    for copy in copies:
        copy.wait()
    stats = [part(b, slice(HEADS_HERE * CAP, RETURNED)) for b in range(NY)]
    shares = []
    for h in range(HEADS_HERE):
        levels = [s[3 * h:3 * h + 1] + s[3 * h + 1:3 * h + 2] + s[3 * h + 2:3 * h + 3] for s in stats]
        top = levels[0]
        for level in levels[1:]:
            top = jnp.maximum(top, level)
        weights = [jnp.exp2(level - top) for level in levels]
        total = weights[0]
        for weight in weights[1:]:
            total = total + weight
        shares += [weight / total for weight in weights]
    shares = jnp.concatenate(shares + [jnp.zeros((HD - len(shares), HD), f32)], axis=0).T
    heads = []
    for h in range(HEADS_HERE):
        accum = jnp.zeros((CAP, HD), f32)
        for b in range(NY):
            share = shares[:CAP, h * NY + b:h * NY + b + 1]
            accum = accum + share * part(b, slice(h * CAP, (h + 1) * CAP))
        heads.append(accum.astype(bf16))
    attended = jnp.concatenate(heads, axis=1)
    half = D // 2
    step = 384
    mask = lower_half((8, step))
    for j in range(half // step):
        left = jnp.dot(attended, w_ref[:, j * step:(j + 1) * step], preferred_element_type=f32)
        right = jnp.dot(attended, w_ref[:, half + j * step:half + (j + 1) * step], preferred_element_type=f32)
        for s in range(NHEAD):
            k = s // 2
            a = left[64 + 8 * k:72 + 8 * k]
            b = right[64 + 8 * k:72 + 8 * k]
            if s % 2 == 0:
                rest = jnp.where(mask, a, pltpu.roll(b, 4, 0))
            else:
                rest = jnp.where(mask, pltpu.roll(a, 4, 0), b)
            pieces = (
                (j * step, left[8 * s:8 * s + 8]),
                (half + j * step, right[8 * s:8 * s + 8]),
                (D + j * step, rest),
            )
            for col, tile in pieces:
                row = 8 * (col // OUT_PACKED)
                col = col % OUT_PACKED
                assert col + step <= OUT_PACKED
                out_ref[s, row:row + 8, col:col + step] = tile.astype(bf16)


def project(parts, own, w):
    return pl.pallas_call(
        project_kernel,
        in_specs=[pl.BlockSpec(memory_space=pltpu.HBM)] * 2 + [pl.BlockSpec(memory_space=pltpu.VMEM)],
        out_specs=pl.BlockSpec(memory_space=pltpu.VMEM),
        out_shape=jax.ShapeDtypeStruct((NHEAD, 16, OUT_PACKED), bf16),
        scratch_shapes=[
            pltpu.VMEM((NY, RETURNED, HD), bf16), pltpu.VMEM((RETURNED, HD), bf16),
            pltpu.SemaphoreType.DMA((2,)),
        ],
        compiler_params=params(24),
    )(parts, own, w)


def mix_kernel(live_ref, in_ref, hidden_ref, gate_ref, out_ref):
    total = in_ref[0].astype(f32)
    for s in range(1, NHEAD):
        total = total + in_ref[s].astype(f32)
    flat = jnp.concatenate([total[0:8], total[8:16]], axis=1)
    half = D // 2
    rest = flat[:, D:]
    tail = jnp.concatenate([rest[0:4], rest[4:8]], axis=1)
    projected = jnp.concatenate([flat[:, :D], tail], axis=0)
    residual = hidden_ref[...].astype(f32)
    live = live_ref[:OWN, :1] > 0.5
    mixed = jnp.where(live, residual + gate_ref[...] * projected, residual)
    out_ref[...] = mixed.astype(bf16)


def mix(live, received, hidden, gate):
    vmem = pl.BlockSpec(memory_space=pltpu.VMEM)
    return pl.pallas_call(
        mix_kernel,
        in_specs=[vmem] * 4,
        out_specs=vmem,
        out_shape=jax.ShapeDtypeStruct((OWN, D), bf16),
        compiler_params=params(16),
    )(live, received, hidden, gate)


def swap(x, axis):
    return lax.all_to_all(x, axis, split_axis=0, concat_axis=0, tiled=True)


def local(fq, fk, fv, sk, sv, lengths, hidden, gate, w):
    kv = lax.all_gather(jnp.concatenate([sk, sv], axis=1), ("z", "c"), axis=0, tiled=True)
    query, kf, vf, bias, live = unpack(lengths, swap(pack(fq, fk, fv), HEAD))
    queries = lax.all_gather(query, "yh", axis=0)
    returned = swap(attend_others(queries, kv, bias), "yh")
    own, staged = attend_own(query, kv, kf, vf, bias, w)
    packed = project(returned, own, staged)
    return mix(live, swap(packed, HEAD), hidden, gate[None, :])


def solution(mesh):
    grid = Mesh(mesh.devices.reshape(NZ, NY, NC, NYL, NX), ALL)
    rows = P(ALL, None)
    stale = P(("z", "yh", "c"), HEAD)
    in_specs = (rows, rows, rows, stale, stale, P(), rows, P(), P(HEAD, None))
    return jax.shard_map(local, mesh=grid, in_specs=in_specs, out_specs=rows, check_vma=False)
```

```python
import jax
import jax.numpy as jnp
import numpy as np
from jax import lax
from jax.experimental import pallas as pl
from jax.experimental.pallas import tpu as pltpu
from jax.sharding import Mesh, PartitionSpec as P

HD = 128
CAP = 96
NZ, NY, NC, NYL, NX = 8, 4, 2, 2, 4
NHEAD = NYL * NX
GROUP = 512
HEADS_HERE = GROUP // HD
OWN = 12
D = 3072
KEYS = NZ * NC * CAP
QUERIES = NY * CAP
BIG = -1e30
TOGETHER = 2
STAT_ROWS = 16
RETURNED = HEADS_HERE * CAP + STAT_ROWS
EXP2_SCALE = float(np.log2(np.e) * HD ** (-0.5))
HEAD = ("yl", "x")
ALL = ("z", "yh", "c", "yl", "x")
f32 = jnp.float32
bf16 = jnp.bfloat16
PACKED = 3 * 768 // 2
OUT_PACKED = (D + D // 2) // 2


def params(mb):
    return pltpu.CompilerParams(vmem_limit_bytes=mb * 2**20)


def lower_half(shape):
    return lax.broadcasted_iota(jnp.int32, shape, 0) < 4


def pack_kernel(q_ref, k_ref, v_ref, out_ref):
    mask = lower_half((8, GROUP // 2))
    for h in range(NHEAD):
        tops, rests = [], []
        for ref in (q_ref, k_ref, v_ref):
            rows = ref[:, h * GROUP:(h + 1) * GROUP].astype(f32)
            tops.append(rows[0:8])
            tail = rows[4:12]
            first = pltpu.roll(tail[:, : GROUP // 2], 4, 0)
            rests.append(jnp.where(mask, first, tail[:, GROUP // 2:]))
        flat = jnp.concatenate(tops + rests, axis=1)
        both = jnp.concatenate([flat[:, :PACKED], flat[:, PACKED:]], axis=0)
        out_ref[h] = both.astype(bf16)


def pack(fq, fk, fv):
    return pl.pallas_call(
        pack_kernel,
        out_shape=jax.ShapeDtypeStruct((NHEAD, 16, PACKED), bf16),
        compiler_params=params(60),
    )(fq, fk, fv)


def unpack_kernel(lengths_ref, in_ref, q_ref, k_ref, v_ref, bias_ref, live_ref):
    mask = lower_half((8, GROUP // 2))
    tops = [[], [], []]
    rests = [[], [], []]
    for s in range(NHEAD):
        both = in_ref[s].astype(f32)
        flat = jnp.concatenate([both[0:8], both[8:16]], axis=1)
        for i in range(3):
            tops[i].append(flat[:, i * GROUP:(i + 1) * GROUP])
            base = 3 * GROUP + i * (GROUP // 2)
            rests[i].append(flat[:, base:base + GROUP // 2])
    for i, ref in enumerate((q_ref, k_ref, v_ref)):
        tiles = list(tops[i])
        for k in range(NHEAD // 2):
            a, b = rests[i][2 * k], rests[i][2 * k + 1]
            left = jnp.where(mask, a, pltpu.roll(b, 4, 0))
            right = jnp.where(mask, pltpu.roll(a, 4, 0), b)
            tiles.append(jnp.concatenate([left, right], axis=1))
        ref[...] = jnp.concatenate(tiles, axis=0).astype(bf16)

    z, yh, c = (lax.axis_index(a) for a in ("z", "yh", "c"))
    row = lax.broadcasted_iota(jnp.int32, (CAP, HD), 0)
    mine = lax.broadcasted_iota(jnp.int32, (CAP, HD), 1) == 1
    for j in range(NZ * NC):
        length = lengths_ref[(j // NC) * NY * NC + yh * NC + j % NC]
        hidden_length = jnp.where((j // NC == z) & (j % NC == c), 0, length)
        seen = row < jnp.where(mine, hidden_length, length)
        bias_ref[j * CAP:(j + 1) * CAP] = jnp.where(seen, 0.0, BIG).astype(bf16)
    rest = row - 64
    token = jnp.where(row < 64, 12 * (row >> 3) + (row & 7), 12 * (rest >> 2) + 8 + (rest & 3))
    own_length = lengths_ref[z * NY * NC + yh * NC + c]
    seen = token < jnp.where(mine, own_length, 0)
    bias_ref[KEYS:] = jnp.where(seen, 0.0, BIG).astype(bf16)
    first = (lax.axis_index("yl") * NX + lax.axis_index("x")) * OWN
    slot = first + lax.broadcasted_iota(jnp.int32, (16, HD), 0)
    live_ref[...] = jnp.where(slot < own_length, 1.0, 0.0)


def unpack(lengths, received):
    one = jax.ShapeDtypeStruct((CAP, GROUP), bf16)
    smem = pl.BlockSpec(memory_space=pltpu.SMEM)
    vmem = pl.BlockSpec(memory_space=pltpu.VMEM)
    return pl.pallas_call(
        unpack_kernel,
        in_specs=[smem, vmem],
        out_specs=(vmem,) * 5,
        out_shape=(
            one, one, one,
            jax.ShapeDtypeStruct((KEYS + CAP, HD), bf16), jax.ShapeDtypeStruct((16, HD), f32),
        ),
        compiler_params=params(16),
    )(lengths, received)


def attend(load_query, keys, hot_lane, count):
    rows = count * CAP
    hot = (lax.broadcasted_iota(jnp.int32, (rows, HD), 1) == hot_lane).astype(f32).astype(bf16)
    query = jnp.concatenate([load_query, hot], axis=1)
    scores = []
    for key, _, bias in keys:
        key = jnp.concatenate([key, bias], axis=1)
        scores.append(lax.dot_general(query, key, (((1,), (1,)), ((), ())), preferred_element_type=f32))
    top = scores[0].max(axis=1, keepdims=True)
    for s in scores[1:]:
        top = jnp.maximum(top, s.max(axis=1, keepdims=True))
    total = jnp.zeros((rows, 1), f32)
    accum = jnp.zeros((rows, HD), f32)
    for s, (_, value, _) in zip(scores, keys):
        weights = jnp.exp2((s - top) * EXP2_SCALE)
        total = total + weights.sum(axis=1, keepdims=True)
        accum = accum + jnp.dot(weights.astype(bf16), value, preferred_element_type=f32)
    return (accum / total).astype(bf16), top * EXP2_SCALE + jnp.log2(total)


def add_stat(stat, level, h):
    lane = lax.broadcasted_iota(jnp.int32, stat.shape, 1)
    hi = level.astype(bf16).astype(f32)
    mid = (level - hi).astype(bf16).astype(f32)
    low = level - hi - mid
    stat = jnp.where(lane == 3 * h, hi, stat)
    stat = jnp.where(lane == 3 * h + 1, mid, stat)
    return jnp.where(lane == 3 * h + 2, low, stat)


def stale_pieces(k_ref, v_ref, bias_ref, cols, parts=4):
    chunk = KEYS // parts
    return [
        (k_ref[j:j + chunk, cols], v_ref[j:j + chunk, cols], bias_ref[j:j + chunk])
        for j in range(0, KEYS, chunk)
    ]


def stat_rows(stat):
    square = jnp.concatenate([stat, jnp.zeros((HD - CAP, HD), f32)], axis=0)
    return square.T[:STAT_ROWS].astype(bf16)


def collect(stat_ref, stat, finish):
    g = pl.program_id(0)

    @pl.when(g == 0)
    def _():
        stat_ref[...] = stat

    @pl.when(g != 0)
    def _():
        stat_ref[...] = stat_ref[...] + stat

    pl.when(g == pl.num_programs(0) - 1)(finish)


def others_kernel(q_hbm, kv_hbm, bias_hbm, out_ref, q_ref, k_ref, v_ref, bias_ref, sems):
    copies = [
        pltpu.make_async_copy(kv_hbm.at[:, :GROUP], k_ref, sems.at[0]),
        pltpu.make_async_copy(kv_hbm.at[:, GROUP:], v_ref, sems.at[1]),
        pltpu.make_async_copy(q_hbm, q_ref, sems.at[2]),
        pltpu.make_async_copy(bias_hbm, bias_ref, sems.at[3]),
    ]
    for copy in copies:
        copy.start()
    yh = lax.axis_index("yh")
    count = NY - 1
    slots = [lax.rem(yh + k, NY) for k in range(1, NY)]
    stat = jnp.zeros((count * CAP, HD), f32)
    out_ref[yh] = jnp.zeros((RETURNED, HD), bf16)
    for copy in copies:
        copy.wait()
    for h in range(HEADS_HERE):
        cols = slice(h * HD, (h + 1) * HD)
        query = jnp.concatenate([q_ref[slot, :, cols] for slot in slots], axis=0)
        result, level = attend(query, stale_pieces(k_ref, v_ref, bias_ref, cols, 3), 0, count)
        for n, slot in enumerate(slots):
            out_ref[slot, h * CAP:(h + 1) * CAP, :] = result[n * CAP:(n + 1) * CAP]
        stat = add_stat(stat, level, h)
    for n, slot in enumerate(slots):
        out_ref[slot, HEADS_HERE * CAP:, :] = stat_rows(stat[n * CAP:(n + 1) * CAP])


def own_kernel(q_ref, k_ref, v_ref, kf_ref, vf_ref, bias_ref, w_ref, out_ref, staged_ref, stat_ref, sem):
    g = pl.program_id(0)
    copy = pltpu.make_async_copy(w_ref, staged_ref, sem)

    @pl.when(g == 0)
    def _():
        copy.start()

    stat = jnp.zeros((CAP, HD), f32)
    for i in range(TOGETHER):
        cols = slice(i * HD, (i + 1) * HD)
        pieces = stale_pieces(k_ref, v_ref, bias_ref, cols)
        pieces.append((kf_ref[:, cols], vf_ref[:, cols], bias_ref[KEYS:]))
        result, level = attend(q_ref[:, cols], pieces, 1, 1)
        h = g * TOGETHER + i
        out_ref[pl.ds(pl.multiple_of(h * CAP, 32), CAP), :] = result
        stat = add_stat(stat, level, h)

    def finish():
        out_ref[HEADS_HERE * CAP:, :] = stat_rows(stat_ref[...])
        copy.wait()

    collect(stat_ref, stat, finish)


STEPS = HEADS_HERE // TOGETHER


def column(rows, skip=0):
    return pl.BlockSpec((rows, TOGETHER * HD), lambda g: (0, g + skip))


def whole(*shape):
    return pl.BlockSpec(shape, lambda g: (0,) * len(shape))


def cost(rows, keys):
    return pl.CostEstimate(
        flops=4 * rows * keys * GROUP,
        bytes_accessed=4 * keys * GROUP,
        transcendentals=rows * keys * HEADS_HERE,
    )


def attend_others(q, kv, bias):
    return pl.pallas_call(
        others_kernel,
        in_specs=[pl.BlockSpec(memory_space=pl.ANY), pl.BlockSpec(memory_space=pltpu.HBM), pl.BlockSpec(memory_space=pl.ANY)],
        out_specs=pl.BlockSpec(memory_space=pltpu.VMEM),
        out_shape=jax.ShapeDtypeStruct((NY, RETURNED, HD), bf16),
        scratch_shapes=[
            pltpu.VMEM((NY, CAP, GROUP), bf16),
            pltpu.VMEM((KEYS, GROUP), bf16), pltpu.VMEM((KEYS, GROUP), bf16),
            pltpu.VMEM((KEYS + CAP, HD), bf16),
            pltpu.SemaphoreType.DMA((4,)),
        ],
        compiler_params=params(60),
        cost_estimate=cost((NY - 1) * CAP, KEYS),
    )(q, kv, bias)


def attend_own(q, kv, kf, vf, bias, w):
    return pl.pallas_call(
        own_kernel,
        grid=(STEPS,),
        in_specs=[
            column(CAP), column(KEYS), column(KEYS, STEPS), column(CAP), column(CAP), whole(KEYS + CAP, HD),
            pl.BlockSpec(memory_space=pltpu.HBM),
        ],
        out_specs=(whole(RETURNED, HD), pl.BlockSpec(memory_space=pl.ANY)),
        out_shape=(pltpu.HBM((RETURNED, HD), bf16), pltpu.VMEM((GROUP, D), bf16)),
        scratch_shapes=[pltpu.VMEM((CAP, HD), f32), pltpu.SemaphoreType.DMA],
        compiler_params=params(56),
        cost_estimate=cost(CAP, KEYS + CAP),
    )(q, kv, kv, kf, vf, bias, w)


def project_kernel(part_hbm, own_hbm, w_ref, out_ref, part_ref, own_ref, sems):
    copies = [
        pltpu.make_async_copy(part_hbm, part_ref, sems.at[0]),
        pltpu.make_async_copy(own_hbm, own_ref, sems.at[1]),
    ]
    for copy in copies:
        copy.start()
    yh = lax.axis_index("yh")

    def part(b, rows):
        return jnp.where(yh == b, own_ref[rows, :].astype(f32), part_ref[b, rows, :].astype(f32))

    for copy in copies:
        copy.wait()
    stats = [part(b, slice(HEADS_HERE * CAP, RETURNED)) for b in range(NY)]
    shares = []
    for h in range(HEADS_HERE):
        levels = [s[3 * h:3 * h + 1] + s[3 * h + 1:3 * h + 2] + s[3 * h + 2:3 * h + 3] for s in stats]
        top = levels[0]
        for level in levels[1:]:
            top = jnp.maximum(top, level)
        weights = [jnp.exp2(level - top) for level in levels]
        total = weights[0]
        for weight in weights[1:]:
            total = total + weight
        shares += [weight / total for weight in weights]
    shares = jnp.concatenate(shares + [jnp.zeros((HD - len(shares), HD), f32)], axis=0).T
    heads = []
    for h in range(HEADS_HERE):
        accum = jnp.zeros((CAP, HD), f32)
        for b in range(NY):
            share = shares[:CAP, h * NY + b:h * NY + b + 1]
            accum = accum + share * part(b, slice(h * CAP, (h + 1) * CAP))
        heads.append(accum.astype(bf16))
    attended = jnp.concatenate(heads, axis=1)
    half = D // 2
    step = 384
    mask = lower_half((8, step))
    for j in range(half // step):
        left = jnp.dot(attended, w_ref[:, j * step:(j + 1) * step], preferred_element_type=f32)
        right = jnp.dot(attended, w_ref[:, half + j * step:half + (j + 1) * step], preferred_element_type=f32)
        for s in range(NHEAD):
            k = s // 2
            a = left[64 + 8 * k:72 + 8 * k]
            b = right[64 + 8 * k:72 + 8 * k]
            if s % 2 == 0:
                rest = jnp.where(mask, a, pltpu.roll(b, 4, 0))
            else:
                rest = jnp.where(mask, pltpu.roll(a, 4, 0), b)
            pieces = (
                (j * step, left[8 * s:8 * s + 8]),
                (half + j * step, right[8 * s:8 * s + 8]),
                (D + j * step, rest),
            )
            for col, tile in pieces:
                row = 8 * (col // OUT_PACKED)
                col = col % OUT_PACKED
                assert col + step <= OUT_PACKED
                out_ref[s, row:row + 8, col:col + step] = tile.astype(bf16)


def project(parts, own, w):
    return pl.pallas_call(
        project_kernel,
        in_specs=[pl.BlockSpec(memory_space=pltpu.HBM)] * 2 + [pl.BlockSpec(memory_space=pltpu.VMEM)],
        out_specs=pl.BlockSpec(memory_space=pltpu.VMEM),
        out_shape=jax.ShapeDtypeStruct((NHEAD, 16, OUT_PACKED), bf16),
        scratch_shapes=[
            pltpu.VMEM((NY, RETURNED, HD), bf16), pltpu.VMEM((RETURNED, HD), bf16),
            pltpu.SemaphoreType.DMA((2,)),
        ],
        compiler_params=params(58),
    )(parts, own, w)


def mix_kernel(live_ref, in_ref, hidden_ref, gate_ref, out_ref):
    total = in_ref[0].astype(f32)
    for s in range(1, NHEAD):
        total = total + in_ref[s].astype(f32)
    flat = jnp.concatenate([total[0:8], total[8:16]], axis=1)
    half = D // 2
    rest = flat[:, D:]
    tail = jnp.concatenate([rest[0:4], rest[4:8]], axis=1)
    projected = jnp.concatenate([flat[:, :D], tail], axis=0)
    residual = hidden_ref[...].astype(f32)
    live = live_ref[:OWN, :1] > 0.5
    mixed = jnp.where(live, residual + gate_ref[...] * projected, residual)
    out_ref[...] = mixed.astype(bf16)


def mix(live, received, hidden, gate):
    vmem = pl.BlockSpec(memory_space=pltpu.VMEM)
    return pl.pallas_call(
        mix_kernel,
        in_specs=[vmem] * 4,
        out_specs=vmem,
        out_shape=jax.ShapeDtypeStruct((OWN, D), bf16),
        compiler_params=params(16),
    )(live, received, hidden, gate)


def swap(x, axis):
    return lax.all_to_all(x, axis, split_axis=0, concat_axis=0, tiled=True)


def local(fq, fk, fv, sk, sv, lengths, hidden, gate, w):
    kv = lax.all_gather(jnp.concatenate([sk, sv], axis=1), ("z", "c"), axis=0, tiled=True)
    query, kf, vf, bias, live = unpack(lengths, swap(pack(fq, fk, fv), HEAD))
    queries = lax.all_gather(query, "yh", axis=0)
    returned = swap(attend_others(queries, kv, bias), "yh")
    own, staged = attend_own(query, kv, kf, vf, bias, w)
    packed = project(returned, own, staged)
    return mix(live, swap(packed, HEAD), hidden, gate[None, :])


def solution(mesh):
    grid = Mesh(mesh.devices.reshape(NZ, NY, NC, NYL, NX), ALL)
    rows = P(ALL, None)
    stale = P(("z", "yh", "c"), HEAD)
    in_specs = (rows, rows, rows, stale, stale, P(), rows, P(), P(HEAD, None))
    return jax.shard_map(local, mesh=grid, in_specs=in_specs, out_specs=rows, check_vma=False)
```
